256 devices in a mesh: gx: 8 (over x, core), gy: 8 (over z), gz: 4 (over y).
Axes of the slice: x: 4, y: 4, z: 8, core: 2. Of those that a mesh axis runs over, the one named last changes fastest.
Arguments:
- spectrum: bfloat16 [256, 256, 32, 256], P('gx', 'gy', 'gz'), may hold values from 0.049804688 to 2
- wind_east: float32 [256, 256, 32], P('gx', 'gy', 'gz'), may hold values from -0.45 to 0.45
- wind_north: float32 [256, 256, 32], P('gx', 'gy', 'gz'), may hold values from -0.45 to 0.45
- fall_rate: float32 [32, 256], P('gz'), may hold values from 0.006 to 12
- cloud_cells: int32 [8, 8, 4, 64, 16], P('gx', 'gy', 'gz'), may hold values from 0 to 8191, as said below
- block_target: int32 [8, 8, 4, 64], P(None, None, 'gz'), may hold values from 0 to 64, as said below
- pair_inputs: bfloat16 [256, 2048], replicated, may hold values from -0.375 to 0.375
- pair_outputs: bfloat16 [1024, 256], replicated, may hold values from -0.1875 to 0.1875
- loss_kernel: bfloat16 [256, 256], replicated, may hold values from 0 to 0.00390625
- fragments: bfloat16 [256, 256], replicated, may hold values from 0 to 0.0078125
Outputs:
- settled: bfloat16 [256, 256, 32, 256], P('gx', 'gy', 'gz')
The draws below stay inside these ranges and needn't reach their ends.
Inputs may be any that keep to these rules, and one draw needn't show every extreme that they name: `cloud_cells`: entry [i, j, k, b, :] lists the local cell numbers (x * 32 + y) * 8 + z of block b of the device at mesh index (i, j, k); the 1024 entries of one device are distinct. `block_target`: entry [i, j, k, b] below 64 is the flat index i2 * (devices along gy) + j2 of the device (i2, j2, k) that works on block b of device (i, j, k); 64 marks a block without cloud. In each gz index the cloudy blocks number 64 * 32 in all, a device holds 1 to 64 of them, every device of the plane is named exactly 32 times, and by at most 1 block of any one device.
All inputs are finite; a program needn't handle non-finite values.
Results may differ from the reference program's by a relative error of at most 0.0032.
Values may be sent and summed in bfloat16 or wider, within the bound.
No kernel may reach another device: no remote copies, remote signals or barrier semaphores. Data moves between devices by JAX's collectives and lax.ppermute only.
A program may use at most 128 MiB of HBM per device.

```python
import math
import jax
import jax.numpy as jnp
from jax import lax

SB = 256
PAIRS = 1024
CX = 32
CY = 32
CZ = 8
NB = 64
BLK = 16
RCAP = 32
PLANE = 64
NX = 256
NY = 256
NZ = 32
N_GX = 8
N_GY = 8
N_GZ = 4


def draw_fall_rate(key, part):
    keys = jax.random.split(jax.random.fold_in(key, 17), 4)
    terminal_speeds = jnp.exp(jax.random.uniform(keys[0], (SB,), jnp.float32, math.log(0.01), math.log(1.5)))
    air_density = jax.random.uniform(keys[1], (NZ, 1), jnp.float32, 0.8, 1.25)
    skipped_levels = jax.random.randint(keys[2], (3,), 0, NZ)
    vertical_levels = jnp.arange(NZ)
    breakup_events = 1.0 + 1.5 * jnp.sum((vertical_levels[:, None] == skipped_levels[None, :]).astype(jnp.float32), axis=1, keepdims=True)
    random_perturbation = jax.random.uniform(keys[3], (NZ, SB), jnp.float32, 0.85, 1.15)
    return (terminal_speeds[None, :] * air_density * breakup_events * random_perturbation).astype(jnp.float32)


def draw_cloud_cells(key, part):
    keys = jax.random.split(jax.random.fold_in(key, 3), N_GX * N_GY * N_GZ)

    def one_device(device_key):
        return jax.random.permutation(device_key, CX * CY * CZ)[:NB * BLK].astype(jnp.int32)
    listed = jax.vmap(one_device)(keys)
    return listed.reshape(N_GX, N_GY, N_GZ, NB, BLK)


def draw_block_target(key, part):
    plane_size = N_GX * N_GY
    total = plane_size * RCAP
    leftover = total - NB
    quota = leftover // (plane_size - 1)
    spare = leftover % (plane_size - 1)
    slope = (quota - 1) // (plane_size - 2)
    base_key = jax.random.fold_in(key, 5)

    def one_plane(plane_index):
        plane_key = jax.random.fold_in(base_key, plane_index)
        keys = jax.random.split(plane_key, 5)
        centre_row = jax.random.randint(keys[0], (), 0, N_GX)
        centre_column = jax.random.randint(keys[1], (), 0, N_GY)
        devices = jnp.arange(plane_size, dtype=jnp.int32)
        distance = jnp.abs(devices // N_GY - centre_row) + jnp.abs(devices % N_GY - centre_column)
        breaker = jax.random.permutation(keys[2], plane_size).astype(jnp.int32)
        scores = distance * plane_size + breaker
        ranking = jnp.argsort(jnp.argsort(scores)).astype(jnp.int32)
        loads = jnp.where(ranking == 0, NB, quota + slope * (plane_size - 2 * ranking) + (ranking - 1 < spare).astype(jnp.int32))
        starts = jnp.cumsum(loads) - loads
        device_keys = jax.random.split(keys[3], plane_size)
        logical = jax.vmap(lambda device_key: jax.random.permutation(device_key, NB).astype(jnp.int32))(device_keys)
        active = logical < loads[:, None]
        spread_target = (starts[:, None] + logical) % plane_size
        relabel = jax.random.permutation(keys[4], plane_size).astype(jnp.int32)
        return jnp.where(active, relabel[spread_target], plane_size).astype(jnp.int32)
    planes = jax.vmap(one_plane)(jnp.arange(N_GZ, dtype=jnp.int32))
    return planes.transpose(1, 0, 2).reshape(N_GX, N_GY, N_GZ, NB)


def block_scale(rng, dims, shards, smallest, largest):
    level, own = 1.0, jax.random.fold_in(rng, 6)
    for axis_at, parts in shards:
        heights = jnp.exp(jax.random.uniform(jax.random.fold_in(own, axis_at), (parts,), jnp.float32, smallest / len(shards), largest / len(shards)))
        level = level * jnp.repeat(heights, dims[axis_at] // parts).reshape([-1 if axis == axis_at else 1 for axis in range(len(dims))])
    return level


def noise(key, extent, spread, bound, held_as=jnp.bfloat16):
    return jnp.clip(spread * jax.random.normal(key, extent, jnp.float32), -bound, bound).astype(held_as)


def setup_inputs(seed: int = 0) -> dict:
    splits = jax.random.split(jax.random.key(seed), 11)
    return {
        "spectrum": jnp.clip(0.049804688 + 1.9501953 * jax.random.uniform(splits[0], (NX, NY, NZ, SB), jnp.float32) ** block_scale(splits[0], (NX, NY, NZ, SB), ((0, 8), (1, 8), (2, 4)), -0.2, 0.2), 0.049804688, 2.0).astype(jnp.bfloat16),
        "wind_east": jnp.clip(jax.random.uniform(splits[1], (NX, NY, NZ), jnp.float32, -0.45, 0.45) * block_scale(splits[1], (NX, NY, NZ), ((0, 8), (1, 8), (2, 4)), -0.4, 0.0), -0.45, 0.45),
        "wind_north": jnp.clip(jax.random.uniform(splits[2], (NX, NY, NZ), jnp.float32, -0.45, 0.45) * block_scale(splits[2], (NX, NY, NZ), ((0, 8), (1, 8), (2, 4)), -0.4, 0.0), -0.45, 0.45),
        "fall_rate": draw_fall_rate(jax.random.fold_in(splits[10], 71), 0),
        "cloud_cells": draw_cloud_cells(jax.random.fold_in(splits[10], 71), 0),
        "block_target": draw_block_target(jax.random.fold_in(splits[10], 71), 0),
        "pair_inputs": noise(splits[6], (SB, 2 * PAIRS), SB ** -0.5, 0.375),
        "pair_outputs": noise(splits[7], (PAIRS, SB), PAIRS ** -0.5, 0.1875),
        "loss_kernel": jnp.clip(jax.random.uniform(splits[8], (SB, SB), jnp.float32, 0.0, 0.00390625), 0.0, 0.00390625).astype(jnp.bfloat16),
        "fragments": jnp.clip(jax.random.uniform(splits[9], (SB, SB), jnp.float32, 0.0, 0.0078125), 0.0, 0.0078125).astype(jnp.bfloat16),
    }


def collide(cloud_rows, pair_inputs, pair_outputs, loss_kernel, fragments):
    pair_count = pair_outputs.shape[0]
    linear = jnp.dot(cloud_rows, pair_inputs, preferred_element_type=jnp.float32)
    products = (linear[:, :pair_count] * linear[:, pair_count:]).astype(jnp.bfloat16)
    decline = jnp.dot(cloud_rows, loss_kernel, preferred_element_type=jnp.float32)
    losses = cloud_rows.astype(jnp.float32) * decline
    gained = jnp.dot(products, pair_outputs, preferred_element_type=jnp.float32)
    gained = gained + jnp.dot(losses.astype(jnp.bfloat16), fragments, preferred_element_type=jnp.float32)
    return (gained - losses).astype(jnp.bfloat16)


def reference(spectrum, wind_east, wind_north, fall_rate, cloud_cells, block_target, pair_inputs, pair_outputs, loss_kernel, fragments):
    def slab_step(slab_index):
        first_level = slab_index * CZ
        values = lax.dynamic_slice_in_dim(spectrum, first_level, CZ, 2).astype(jnp.float32)
        east_rate = lax.dynamic_slice_in_dim(wind_east, first_level, CZ, 2)[..., None]
        north_rate = lax.dynamic_slice_in_dim(wind_north, first_level, CZ, 2)[..., None]
        from_west = jnp.roll(values, 1, 0)
        from_east = jnp.roll(values, -1, 0)
        from_south = jnp.roll(values, 1, 1)
        from_north = jnp.roll(values, -1, 1)
        advected = (values - jnp.maximum(east_rate, 0.0) * (values - from_west)
                    - jnp.minimum(east_rate, 0.0) * (from_east - values)
                    - jnp.maximum(north_rate, 0.0) * (values - from_south)
                    - jnp.minimum(north_rate, 0.0) * (from_north - values))
        targets = lax.dynamic_index_in_dim(block_target, slab_index, 2, keepdims=False).reshape(PLANE * NB)
        listed = lax.dynamic_index_in_dim(cloud_cells, slab_index, 2, keepdims=False).reshape(PLANE * NB, BLK)
        chosen = jnp.argsort((targets >= PLANE).astype(jnp.int32), stable=True)[: PLANE * RCAP].astype(jnp.int32)
        owners = chosen // NB
        tile_row = (owners // N_GY)[:, None]
        tile_column = (owners % N_GY)[:, None]
        local_ids = listed[chosen]
        cell_row = local_ids // (CY * CZ)
        cell_column = (local_ids // CZ) % CY
        cell_level = local_ids % CZ
        global_ids = (((tile_row * CX + cell_row) * NY + tile_column * CY + cell_column) * CZ + cell_level).reshape(-1).astype(jnp.int32)
        flat_values = advected.reshape(NX * NY * CZ, SB)
        gathered = flat_values[global_ids].astype(jnp.bfloat16)
        tendency = collide(gathered, pair_inputs, pair_outputs, loss_kernel, fragments)
        moist_field = flat_values.at[global_ids].add(tendency.astype(jnp.float32))
        return moist_field.reshape(NX, NY, CZ, SB)

    moist_slabs = lax.map(slab_step, jnp.arange(N_GZ, dtype=jnp.int32))
    fall_slabs = fall_rate.reshape(N_GZ, CZ, SB)

    def settle(inflow, pieces):
        moist_field, level_rates = pieces
        layers = [None] * CZ
        for level_index in reversed(range(CZ)):
            level_rate = level_rates[level_index]
            level_value = (moist_field[:, :, level_index] + inflow) / (1.0 + level_rate)
            inflow = level_rate * level_value
            layers[level_index] = level_value.astype(jnp.bfloat16)
        return inflow, jnp.stack(layers, axis=2)

    initial_flow = jnp.zeros((NX, NY, SB), jnp.float32)
    final_flow, settled = lax.scan(settle, initial_flow, (moist_slabs, fall_slabs), reverse=True)
    return settled.transpose(1, 2, 0, 3, 4).reshape(NX, NY, NZ, SB)
```

```python
import jax
import jax.numpy as jnp
from jax import lax
from jax.experimental import pallas as pl
from jax.experimental.pallas import tpu as pltpu
from jax.sharding import PartitionSpec as P

F32 = jnp.float32
BF16 = jnp.bfloat16
GAIN_ROWS = 16
HALVES = 2


def edges_kernel(s_ref, west_ref, east_ref, south_ref, north_ref, sems):
    nx, ny = s_ref.shape[:2]
    pieces = (
        (s_ref.at[0:1], west_ref),
        (s_ref.at[nx - 1 : nx], east_ref),
        (s_ref.at[:, 0:1], south_ref),
        (s_ref.at[:, ny - 1 : ny], north_ref),
    )
    copies = [
        pltpu.make_async_copy(src, dst, sems.at[i]) for i, (src, dst) in enumerate(pieces)
    ]
    for copy in copies:
        copy.start()
    for copy in copies:
        copy.wait()


def edges(spectrum):
    nx, ny, nz, nb = spectrum.shape
    any_spec = pl.BlockSpec(memory_space=pl.ANY)
    row = jax.ShapeDtypeStruct((1, ny, nz, nb), BF16)
    column = jax.ShapeDtypeStruct((nx, 1, nz, nb), BF16)
    return pl.pallas_call(
        edges_kernel,
        out_shape=(row, row, column, column),
        in_specs=[any_spec],
        out_specs=[any_spec] * 4,
        scratch_shapes=[pltpu.SemaphoreType.DMA((4,))],
        compiler_params=pltpu.CompilerParams(vmem_limit_bytes=2**20),
        name="edges",
    )(spectrum)


def cell_kernel(
    cells_ref,
    active_ref,
    s_any,
    west_any,
    east_any,
    south_any,
    north_any,
    we_ref,
    wn_ref,
    fall_ref,
    pi_ref,
    po_ref,
    lk_ref,
    fr_ref,
    local_any,
    flux_ref,
    pad,
    south,
    north,
    adv,
    rows,
    stage,
    sems,
):
    nx, ny, nz, nb = s_any.shape
    blk, blocks = cells_ref.shape
    pairs = po_ref.shape[0]
    tiles = nb // 128
    parts = 4
    per = nx // parts
    ins = [
        pltpu.make_async_copy(west_any, pad.at[0:1], sems.at[0]),
        pltpu.make_async_copy(east_any, pad.at[nx + 1 : nx + 2], sems.at[1]),
        pltpu.make_async_copy(south_any, south, sems.at[2]),
        pltpu.make_async_copy(north_any, north, sems.at[3]),
    ]
    for i in range(parts):
        ins.append(
            pltpu.make_async_copy(
                s_any.at[i * per : (i + 1) * per],
                pad.at[1 + i * per : 1 + (i + 1) * per],
                sems.at[4 + i],
            )
        )
    for copy in ins:
        copy.start()
    for copy in ins:
        copy.wait()

    def advect(x, carry):
        u = we_ref[x]
        v = wn_ref[x]
        c_w = jnp.maximum(u, 0.0)
        c_e = jnp.maximum(-u, 0.0)
        c_s = jnp.maximum(v, 0.0)
        c_n = jnp.maximum(-v, 0.0)
        c_0 = 1.0 - c_w - c_e - c_s - c_n

        def wide(c, y):
            return jnp.broadcast_to(c[:, y : y + 1], (nz, nb))

        behind = south[x, 0].astype(F32)
        here = pad[x + 1, 0].astype(F32)
        for y in range(ny):
            ahead = (north[x, 0] if y == ny - 1 else pad[x + 1, y + 1]).astype(F32)
            value = (
                wide(c_0, y) * here
                + wide(c_w, y) * pad[x, y].astype(F32)
                + wide(c_e, y) * pad[x + 2, y].astype(F32)
                + wide(c_s, y) * behind
                + wide(c_n, y) * ahead
            )
            at = pl.ds(pl.multiple_of(x * (ny * nz) + y * nz, 8), nz)
            for t in range(tiles):
                adv[t, at, :] = value[:, t * 128 : (t + 1) * 128]
            behind, here = here, ahead
        return carry

    lax.fori_loop(0, nx, advect, 0)

    def gather(b, carry):
        base = pl.multiple_of(b * blk, blk)
        for j in range(blk):
            for t in range(tiles):
                rows[t, pl.ds(base + j, 1), :] = adv[t, pl.ds(cells_ref[j, b], 1), :]
        return carry

    lax.fori_loop(0, blocks, gather, 0)

    step = 512
    tile = 256

    def collide(i, carry):
        here = pl.ds(pl.multiple_of(i * step, step), step)
        cloud = jnp.concatenate([rows[t, here, :] for t in range(tiles)], 1).astype(BF16)
        decline = jnp.dot(cloud, lk_ref[...], preferred_element_type=F32)
        losses = cloud.astype(F32) * decline
        total = jnp.dot(losses.astype(BF16), fr_ref[...], preferred_element_type=F32) - losses
        for n in range(pairs // tile):
            left = jnp.dot(
                cloud, pi_ref[:, n * tile : (n + 1) * tile], preferred_element_type=F32
            )
            right = jnp.dot(
                cloud,
                pi_ref[:, pairs + n * tile : pairs + (n + 1) * tile],
                preferred_element_type=F32,
            )
            total = total + jnp.dot(
                (left * right).astype(BF16),
                po_ref[n * tile : (n + 1) * tile, :],
                preferred_element_type=F32,
            )
        total = total.astype(BF16).astype(F32)
        for t in range(tiles):
            rows[t, here, :] = total[:, t * 128 : (t + 1) * 128]
        return carry

    lax.fori_loop(0, blocks * blk // step, collide, 0)

    def scatter(b, carry):
        base = pl.multiple_of(b * blk, blk)

        @pl.when(active_ref[b] != 0)
        def _():
            ids = [cells_ref[j, b] for j in range(blk)]
            sums = [
                adv[t, pl.ds(ids[j], 1), :] + rows[t, pl.ds(base + j, 1), :]
                for j in range(blk)
                for t in range(tiles)
            ]
            for j in range(blk):
                for t in range(tiles):
                    adv[t, pl.ds(ids[j], 1), :] = sums[j * tiles + t]

        return carry

    lax.fori_loop(0, blocks, scatter, 0)

    fall = fall_ref[...]
    inverse = 1.0 / (1.0 + fall)
    through = fall * inverse
    cut = 2 * 8 * nz

    def settle(g, carry):
        base = pl.multiple_of(g * cut, cut)
        flows = []
        for t in range(tiles):
            lanes = slice(t * 128, (t + 1) * 128)
            for half in range(2):
                inflow = jnp.zeros((8, 128), F32)
                for z in reversed(range(nz)):
                    at = pl.ds(base + half * 8 * nz + z, 8, stride=nz)
                    total = adv[t, at, :] + inflow
                    adv[t, at, :] = total * inverse[z : z + 1, lanes]
                    inflow = total * through[z : z + 1, lanes]
                flows.append(inflow)
            flux_ref[pl.ds(pl.multiple_of(g * 16, 16), 16), lanes] = jnp.concatenate(
                flows[-2:], 0
            ).astype(BF16)
        for c in range(16):
            column = pl.ds(pl.multiple_of(base + c * nz, 8), nz)
            stage[g // 2, (g % 2) * 16 + c] = jnp.concatenate(
                [adv[t, column, :] for t in range(tiles)], 1
            ).astype(BF16)
        return carry

    for i in range(parts):
        lax.fori_loop(i * per * 2, (i + 1) * per * 2, settle, 0)
        pltpu.make_async_copy(
            stage.at[i * per : (i + 1) * per],
            local_any.at[i * per : (i + 1) * per],
            sems.at[4 + i],
        ).start()

    gain = jnp.ones((1, nb), F32)
    for z in reversed(range(nz)):
        gain = gain * through[z : z + 1, :]
    flux_ref[pl.ds(nx * ny, GAIN_ROWS), :] = jnp.broadcast_to(gain, (GAIN_ROWS, nb)).astype(BF16)
    for i in range(parts):
        pltpu.make_async_copy(
            stage.at[i * per : (i + 1) * per],
            local_any.at[i * per : (i + 1) * per],
            sems.at[4 + i],
        ).wait()


def combine_kernel(zid_ref, own_ref, a_ref, b_ref, out_ref):
    n = own_ref.shape[0] - GAIN_ROWS
    z = zid_ref[0]

    @pl.when(z == 0)
    def _():
        out_ref[...] = b_ref[...]

    @pl.when(z != 0)
    def _():
        gain = own_ref[n : n + GAIN_ROWS, :].astype(F32)

        def some(i, carry):
            at = pl.ds(pl.multiple_of(i * 16, 16), 16)
            out_ref[at, :] = (
                own_ref[at, :].astype(F32) + gain * a_ref[at, :].astype(F32)
            ).astype(BF16)
            return carry

        lax.fori_loop(0, n // 16, some, 0, unroll=4)
        out_ref[n : n + GAIN_ROWS, :] = (
            gain * a_ref[n : n + GAIN_ROWS, :].astype(F32)
        ).astype(BF16)


def combine(zid, own, a, b):
    vmem = pl.BlockSpec(memory_space=pltpu.VMEM)
    return pl.pallas_call(
        combine_kernel,
        out_shape=jax.ShapeDtypeStruct(own.shape, BF16),
        in_specs=[pl.BlockSpec(memory_space=pltpu.SMEM), vmem, vmem, vmem],
        out_specs=vmem,
        compiler_params=pltpu.CompilerParams(vmem_limit_bytes=4 * 2**20),
        name="combine",
    )(zid, own, a, b)


def finish_kernel(zid_ref, fall_ref, a_ref, b_ref, d_ref, local_ref, out_ref, inflow):
    nxs, ny, nz, nb = local_ref.shape
    n = a_ref.shape[0] - GAIN_ROWS
    rows = nxs * ny
    z = zid_ref[0]
    fall = fall_ref[...]
    through = fall / (1.0 + fall)
    inverse = 1.0 / (1.0 + fall)
    carried = jnp.ones((1, nb), F32)
    gains = [None] * nz
    for level in reversed(range(nz)):
        gains[level] = carried * inverse[level : level + 1, :]
        carried = carried * through[level : level + 1, :]
    gain = jnp.concatenate(gains, 0)
    start = pl.program_id(0) * rows
    bottom = z == 0
    mix = jnp.where(bottom, d_ref[n : n + GAIN_ROWS, :], a_ref[n : n + GAIN_ROWS, :]).astype(F32)
    for i in range(rows // 16):
        at = pl.ds(pl.multiple_of(start + i * 16, 16), 16)
        a, b, d = a_ref[at, :].astype(F32), b_ref[at, :].astype(F32), d_ref[at, :].astype(F32)
        inflow[i * 16 : (i + 1) * 16, :] = jnp.where(bottom, d, a) + mix * jnp.where(bottom, b, d)

    def column(x, carry):
        for y in range(ny):
            m = jnp.broadcast_to(inflow[pl.ds(x * ny + y, 1), :], (nz, nb))
            out_ref[x, y] = (local_ref[x, y].astype(F32) + m * gain).astype(BF16)
        return carry

    lax.fori_loop(0, nxs, column, 0)


def finish(zid, fall, a, b, d, local, half):
    nx, ny, nz, nb = local.shape
    nxs = 4
    steps = nx // HALVES // nxs
    vmem = pl.BlockSpec(memory_space=pltpu.VMEM)
    block = pl.BlockSpec((nxs, ny, nz, nb), lambda i: (i + half * steps, 0, 0, 0))
    return pl.pallas_call(
        finish_kernel,
        out_shape=jax.ShapeDtypeStruct(local.shape, BF16),
        grid=(steps,),
        in_specs=[
            pl.BlockSpec(memory_space=pltpu.SMEM),
            vmem,
            vmem,
            vmem,
            vmem,
            block,
        ],
        out_specs=block,
        scratch_shapes=[pltpu.VMEM((nxs * ny, nb), F32)],
        input_output_aliases={5: 0},
        compiler_params=pltpu.CompilerParams(vmem_limit_bytes=12 * 2**20),
        name="finish",
    )(zid, fall, a, b, d, local)


def cell_work(cells, active, spectrum, halo, we, wn, fall, pi, po, lk, fr):
    nx, ny, nz, nb = spectrum.shape
    vmem = pl.BlockSpec(memory_space=pltpu.VMEM)
    smem = pl.BlockSpec(memory_space=pltpu.SMEM)
    any_spec = pl.BlockSpec(memory_space=pl.ANY)
    blk, blocks = cells.shape
    return pl.pallas_call(
        cell_kernel,
        out_shape=(
            jax.ShapeDtypeStruct(spectrum.shape, BF16),
            jax.ShapeDtypeStruct((nx * ny + GAIN_ROWS, nb), BF16),
        ),
        in_specs=[smem, smem] + [any_spec] * 5 + [vmem] * 7,
        out_specs=(any_spec, vmem),
        scratch_shapes=[
            pltpu.VMEM((nx + 2, ny, nz, nb), BF16),
            pltpu.VMEM((nx, 1, nz, nb), BF16),
            pltpu.VMEM((nx, 1, nz, nb), BF16),
            pltpu.VMEM((nb // 128, nx * ny * nz, 128), F32),
            pltpu.VMEM((nb // 128, blk * blocks, 128), F32),
            pltpu.VMEM((nx, ny, nz, nb), BF16),
            pltpu.SemaphoreType.DMA((8,)),
        ],
        compiler_params=pltpu.CompilerParams(vmem_limit_bytes=40 * 2**20),
        name="cells",
    )(cells, active, spectrum, *halo, we, wn, fall, pi, po, lk, fr)


def body(
    spectrum,
    wind_east,
    wind_north,
    fall_rate,
    cloud_cells,
    block_target,
    pair_inputs,
    pair_outputs,
    loss_kernel,
    fragments,
):
    nx, ny, nz, nb = spectrum.shape
    n_gx, n_gy = (lax.axis_size(a) for a in ("gx", "gy"))
    up_x = [(i, (i + 1) % n_gx) for i in range(n_gx)]
    up_y = [(i, (i + 1) % n_gy) for i in range(n_gy)]
    low_x, high_x, low_y, high_y = edges(spectrum)
    south = lax.ppermute(high_y, "gy", up_y)
    north = lax.ppermute(low_y, "gy", [(b, a) for a, b in up_y])
    west = lax.ppermute(high_x, "gx", up_x)
    east = lax.ppermute(low_x, "gx", [(b, a) for a, b in up_x])

    blocks, blk = cloud_cells.shape[3:]
    cells = cloud_cells.reshape(blocks, blk).T
    plane = n_gx * n_gy
    own = lax.axis_index("gx") * n_gy + lax.axis_index("gy")
    targets = lax.dynamic_index_in_dim(block_target.reshape(plane, blocks), own, 0, keepdims=False)
    active = (targets < plane).astype(jnp.int32)
    local, flux = cell_work(
        cells,
        active,
        spectrum,
        (west, east, south, north),
        wind_east.transpose(0, 2, 1),
        wind_north.transpose(0, 2, 1),
        fall_rate,
        pair_inputs,
        pair_outputs,
        loss_kernel,
        fragments,
    )
    zid = lax.axis_index("gz").reshape(1)
    count = nx * ny // HALVES
    firsts = []
    for h in range(HALVES):
        piece = jnp.concatenate([flux[h * count : (h + 1) * count], flux[nx * ny :]], 0)
        a = lax.ppermute(piece, "gz", [(3, 2), (2, 1)])
        b = lax.ppermute(piece, "gz", [(3, 0)])
        firsts.append((piece, a, b))
    seconds = []
    for piece, a, b in firsts:
        c = combine(zid, piece, a, b)
        d = lax.ppermute(c, "gz", [(1, 0), (0, 1)])
        seconds.append((a, b, d))
    out = local
    for h, (a, b, d) in enumerate(seconds):
        out = finish(zid, fall_rate, a, b, d, out, h)
    return out


def solution(mesh):
    in_specs = (
        P("gx", "gy", "gz", None),
        P("gx", "gy", "gz"),
        P("gx", "gy", "gz"),
        P("gz", None),
        P("gx", "gy", "gz", None, None),
        P(None, None, "gz", None),
        P(),
        P(),
        P(),
        P(),
    )
    out_specs = P("gx", "gy", "gz", None)
    return jax.shard_map(body, mesh=mesh, in_specs=in_specs, out_specs=out_specs, check_vma=False)
```

```python
import functools

import jax
import jax.numpy as jnp
from jax import lax
from jax.experimental import pallas as pl
from jax.experimental.pallas import tpu as pltpu
from jax.sharding import PartitionSpec as P

F32 = jnp.float32
BF16 = jnp.bfloat16
LANES = 128
GROUP = 4
GAIN_ROWS = 16
MIB = 2**20
VMEM = pl.BlockSpec(memory_space=pltpu.VMEM)
SMEM = pl.BlockSpec(memory_space=pltpu.SMEM)
ANY = pl.BlockSpec(memory_space=pl.ANY)
HBM = pl.BlockSpec(memory_space=pltpu.HBM)
in_hbm = functools.partial(pltpu.with_memory_space_constraint, memory_space=pltpu.HBM)
in_vmem = functools.partial(pltpu.with_memory_space_constraint, memory_space=pltpu.VMEM)


def edges_kernel(s_ref, west_ref, east_ref, south_ref, north_ref, sems):
    nx, ny = s_ref.shape[:2]
    pieces = (
        (s_ref.at[0:1], west_ref),
        (s_ref.at[nx - 1 : nx], east_ref),
        (s_ref.at[:, 0:1], south_ref),
        (s_ref.at[:, ny - 1 : ny], north_ref),
    )
    copies = [
        pltpu.make_async_copy(src, dst, sems.at[i]) for i, (src, dst) in enumerate(pieces)
    ]
    for copy in copies:
        copy.start()
    for copy in copies:
        copy.wait()


def edges(spectrum):
    nx, ny, nz, nb = spectrum.shape
    row = jax.ShapeDtypeStruct((1, ny, nz, nb), BF16)
    column = jax.ShapeDtypeStruct((nx, 1, nz, nb), BF16)
    return pl.pallas_call(
        edges_kernel,
        out_shape=(row, row, column, column),
        in_specs=[HBM],
        out_specs=[ANY] * 4,
        scratch_shapes=[pltpu.SemaphoreType.DMA((4,))],
        compiler_params=pltpu.CompilerParams(vmem_limit_bytes=MIB),
        name="edges",
    )(in_hbm(spectrum))


def wide(c, y, shape):
    return jnp.broadcast_to(c[:, y : y + 1], shape)


def inner_kernel(s_any, we_any, wn_any, adv, s_ref, we_ref, wn_ref, sems):
    nx, ny, nz, nb = s_ref.shape
    winds = [
        pltpu.make_async_copy(we_any, we_ref, sems.at[0]),
        pltpu.make_async_copy(wn_any, wn_ref, sems.at[1]),
    ]
    cuts = (0, GROUP + 1, nx // 2 + 1, nx)
    loads = [
        pltpu.make_async_copy(s_any.at[lo:hi], s_ref.at[lo:hi], sems.at[2 + i])
        for i, (lo, hi) in enumerate(zip(cuts, cuts[1:]))
    ]
    for copy in winds + loads:
        copy.start()
    for copy in winds:
        copy.wait()

    half = (nz, LANES)
    none = jnp.zeros((nz, nb), F32)

    def advect(g, carry):
        x = g * GROUP
        before, after = jnp.maximum(x - 1, 0), jnp.minimum(x + GROUP, nx - 1)
        has_before = jnp.where(x > 0, 1.0, 0.0)
        has_after = jnp.where(x + GROUP < nx, 1.0, 0.0)
        us = [we_ref[x + r] for r in range(GROUP)]
        vs = [wn_ref[x + r] for r in range(GROUP)]
        behind = [none] * GROUP
        here = [s_ref[x + r, 0].astype(F32) for r in range(GROUP)]
        for y in range(ny):
            if y < ny - 1:
                ahead = [s_ref[x + r, y + 1].astype(F32) for r in range(GROUP)]
            else:
                ahead = [none] * GROUP
            line = [
                s_ref[before, y].astype(F32) * has_before,
                *here,
                s_ref[after, y].astype(F32) * has_after,
            ]
            for r in range(GROUP):
                u, v = wide(us[r], y, half), wide(vs[r], y, half)
                from_low, from_south = u > 0.0, v > 0.0
                u, v = jnp.abs(u), jnp.abs(v)
                at = pl.ds(pl.multiple_of(((x + r) * ny + y) * nz, 8), nz)
                for t in range(nb // LANES):
                    lanes = slice(t * LANES, (t + 1) * LANES)
                    own = here[r][:, lanes]
                    side = jnp.where(from_low, line[r][:, lanes], line[r + 2][:, lanes])
                    other = jnp.where(from_south, behind[r][:, lanes], ahead[r][:, lanes])
                    adv[t, at, :] = own + u * (side - own) + v * (other - own)
            behind, here = here, ahead
        return carry

    done = 0
    for hi, copy in zip(cuts[1:], loads):
        copy.wait()
        ready = (nx if hi == nx else hi - 1) // GROUP
        lax.fori_loop(done, ready, advect, 0)
        done = ready


def settle_columns(adv, flux_ref, fall, first, count):
    nz, nb = fall.shape
    inverse = 1.0 / (1.0 + fall)
    through = fall * inverse
    tiles = adv.shape[0]

    def settle(g, carry):
        base = pl.multiple_of((first + g * 16) * nz, 128)
        for t in range(tiles):
            lanes = slice(t * LANES, (t + 1) * LANES)
            flows = []
            for half in range(2):
                inflow = jnp.zeros((8, LANES), F32)
                for z in reversed(range(nz)):
                    at = pl.ds(base + half * 8 * nz + z, 8, stride=nz)
                    total = adv[t, at, :] + inflow
                    adv[t, at, :] = total * inverse[z : z + 1, lanes]
                    inflow = total * through[z : z + 1, lanes]
                flows.append(inflow)
            flux_ref[pl.ds(pl.multiple_of(g * 16, 16), 16), lanes] = jnp.concatenate(
                flows, 0
            ).astype(BF16)
        return carry

    lax.fori_loop(0, count // 16, settle, 0)
    gain = jnp.ones((1, nb), F32)
    for z in reversed(range(nz)):
        gain = gain * through[z : z + 1, :]
    flux_ref[pl.ds(count, GAIN_ROWS), :] = jnp.broadcast_to(gain, (GAIN_ROWS, nb)).astype(BF16)


def cloud_kernel(
    place_ref,
    cells_any,
    target_any,
    adv_in,
    west_ref,
    east_ref,
    south_ref,
    north_ref,
    we_ref,
    wn_ref,
    fall_ref,
    pi_ref,
    po_ref,
    lk_ref,
    fr_ref,
    adv,
    flux_ref,
    cells,
    target,
    rows,
    sems,
):
    del adv_in
    nx, nz, ny = we_ref.shape
    nb = fall_ref.shape[1]
    blk, blocks = cells.shape
    pairs = po_ref.shape[0]
    tiles = nb // LANES
    plane = target_any.shape[0] * target_any.shape[1]
    lists = pltpu.make_async_copy(cells_any, cells, sems.at[0])
    routes = pltpu.make_async_copy(target_any.at[place_ref[0], place_ref[1]], target, sems.at[1])
    lists.start()
    routes.start()

    def add(cell, value):
        at = pl.ds(pl.multiple_of(cell, 8), nz)
        for t in range(tiles):
            adv[t, at, :] += value[:, t * LANES : (t + 1) * LANES]

    shape = (nz, nb)
    c_w = jnp.maximum(we_ref[0], 0.0)
    c_e = jnp.maximum(-we_ref[nx - 1], 0.0)
    for y in range(ny):
        add(y * nz, wide(c_w, y, shape) * west_ref[0, y].astype(F32))
        add(((nx - 1) * ny + y) * nz, wide(c_e, y, shape) * east_ref[0, y].astype(F32))

    def sides(i, carry):
        for k in range(4):
            x = i * 4 + k
            v = wn_ref[x]
            c_s = jnp.maximum(v, 0.0)
            c_n = jnp.maximum(-v, 0.0)
            add(x * ny * nz, wide(c_s, 0, shape) * south_ref[x, 0].astype(F32))
            add((x * ny + ny - 1) * nz, wide(c_n, ny - 1, shape) * north_ref[x, 0].astype(F32))
        return carry

    lax.fori_loop(0, nx // 4, sides, 0)
    lists.wait()

    def gather(b, carry):
        base = pl.multiple_of(b * blk, blk)
        for j in range(blk):
            for t in range(tiles):
                rows[t, pl.ds(base + j, 1), :] = adv[t, pl.ds(cells[j, b], 1), :]
        return carry

    lax.fori_loop(0, blocks, gather, 0)

    step = 512
    tile = 256

    def collide(i, carry):
        here = pl.ds(pl.multiple_of(i * step, step), step)
        cloud = jnp.concatenate([rows[t, here, :] for t in range(tiles)], 1).astype(BF16)
        decline = jnp.dot(cloud, lk_ref[...], preferred_element_type=F32)
        losses = cloud.astype(F32) * decline
        total = jnp.dot(losses.astype(BF16), fr_ref[...], preferred_element_type=F32) - losses
        for n in range(pairs // tile):
            left = jnp.dot(
                cloud, pi_ref[:, n * tile : (n + 1) * tile], preferred_element_type=F32
            )
            right = jnp.dot(
                cloud,
                pi_ref[:, pairs + n * tile : pairs + (n + 1) * tile],
                preferred_element_type=F32,
            )
            total = total + jnp.dot(
                (left * right).astype(BF16),
                po_ref[n * tile : (n + 1) * tile, :],
                preferred_element_type=F32,
            )
        total = total.astype(BF16).astype(F32)
        for t in range(tiles):
            rows[t, here, :] += total[:, t * LANES : (t + 1) * LANES]
        return carry

    lax.fori_loop(0, blocks * blk // step, collide, 0)
    routes.wait()

    def scatter(b, carry):
        base = pl.multiple_of(b * blk, blk)

        @pl.when(target[0, b] < plane)
        def _():
            for j in range(blk):
                for t in range(tiles):
                    adv[t, pl.ds(cells[j, b], 1), :] = rows[t, pl.ds(base + j, 1), :]

        return carry

    lax.fori_loop(0, blocks, scatter, 0)
    count = flux_ref.shape[0] - GAIN_ROWS
    settle_columns(adv, flux_ref, fall_ref[...], 0, count)


def settle_kernel(adv, fall_ref, local_any, flux_ref, sems):
    nz = fall_ref.shape[0]
    count = flux_ref.shape[0] - GAIN_ROWS
    first = adv.shape[1] // nz - count
    cut = first * nz
    front = pltpu.make_async_copy(adv.at[:, :cut], local_any.at[:, :cut], sems.at[0])
    back = pltpu.make_async_copy(adv.at[:, cut:], local_any.at[:, cut:], sems.at[1])
    front.start()
    settle_columns(adv, flux_ref, fall_ref[...], first, count)
    back.start()
    front.wait()
    back.wait()


def combine_kernel(zid_ref, own_ref, a_ref, b_ref, out_ref):
    n = own_ref.shape[0] - GAIN_ROWS
    z = zid_ref[0]

    @pl.when(z == 0)
    def _():
        out_ref[...] = b_ref[...]

    @pl.when(z != 0)
    def _():
        gain = own_ref[n : n + GAIN_ROWS, :].astype(F32)

        def some(i, carry):
            at = pl.ds(pl.multiple_of(i * 16, 16), 16)
            out_ref[at, :] = (
                own_ref[at, :].astype(F32) + gain * a_ref[at, :].astype(F32)
            ).astype(BF16)
            return carry

        lax.fori_loop(0, n // 16, some, 0, unroll=4)
        out_ref[n : n + GAIN_ROWS, :] = (
            gain * a_ref[n : n + GAIN_ROWS, :].astype(F32)
        ).astype(BF16)


def combine(zid, own, a, b):
    return pl.pallas_call(
        combine_kernel,
        out_shape=pltpu.VMEM(own.shape, BF16),
        in_specs=[SMEM] + [VMEM] * 3,
        out_specs=VMEM,
        compiler_params=pltpu.CompilerParams(vmem_limit_bytes=4 * MIB),
        name="combine",
    )(zid, own, a, b)


def finish_kernel(
    zid_ref,
    fall_ref,
    a_ref,
    b_ref,
    d_ref,
    local_any,
    prev_ref,
    out_any,
    local,
    inflow,
    stage,
    sems,
    *,
    first,
):
    del prev_ref
    ny, nz, nb = out_any.shape[1:]
    parts, per = stage.shape[:2]
    tiles = nb // LANES
    n = a_ref.shape[0] - GAIN_ROWS
    span = per * ny * nz
    loads = []
    for p in range(parts):
        start = first * ny * nz + p * span
        loads.append(
            pltpu.make_async_copy(
                local_any.at[:, start : start + span],
                local.at[:, p * span : (p + 1) * span],
                sems.at[p],
            )
        )
        loads[-1].start()
    fall = fall_ref[...]
    inverse = 1.0 / (1.0 + fall)
    through = fall * inverse
    carried = jnp.ones((1, nb), F32)
    gains = [None] * nz
    for level in reversed(range(nz)):
        gains[level] = carried * inverse[level : level + 1, :]
        carried = carried * through[level : level + 1, :]
    gain = jnp.concatenate(gains, 0)
    bottom = zid_ref[0] == 0
    mix = jnp.where(bottom, d_ref[n : n + GAIN_ROWS, :], a_ref[n : n + GAIN_ROWS, :]).astype(F32)

    def enter(i, carry):
        at = pl.ds(pl.multiple_of(i * 16, 16), 16)
        a, b, d = a_ref[at, :].astype(F32), b_ref[at, :].astype(F32), d_ref[at, :].astype(F32)
        inflow[at, :] = jnp.where(bottom, d, a) + mix * jnp.where(bottom, b, d)
        return carry

    lax.fori_loop(0, n // 16, enter, 0, unroll=4)
    copies = []
    for p in range(parts):

        def column(x, carry, p=p):
            base = (p * per + x) * ny
            for y in range(ny):
                at = pl.ds(pl.multiple_of((base + y) * nz, 8), nz)
                m = jnp.broadcast_to(inflow[pl.ds(base + y, 1), :], (nz, nb))
                own = jnp.concatenate([local[t, at, :] for t in range(tiles)], 1)
                stage[p, x, y] = (own + m * gain).astype(BF16)
            return carry

        loads[p].wait()
        lax.fori_loop(0, per, column, 0)
        copy = pltpu.make_async_copy(
            stage.at[p], out_any.at[first + p * per : first + (p + 1) * per], sems.at[p]
        )
        copy.start()
        copies.append(copy)
    for copy in copies:
        copy.wait()


def finish(zid, fall, a, b, d, local, prev, shape, first, parts):
    nx, ny, nz, nb = shape
    n = a.shape[0] - GAIN_ROWS
    given = (zid, fall, a, b, d, in_hbm(local)) + (() if prev is None else (prev,))
    kernel = functools.partial(finish_kernel, first=first)
    if prev is None:
        inner = kernel

        def kernel(*refs):
            return inner(*refs[:6], None, *refs[6:])

    return pl.pallas_call(
        kernel,
        out_shape=jax.ShapeDtypeStruct(shape, BF16),
        in_specs=[SMEM] + [VMEM] * 4 + [HBM] + [ANY] * (prev is not None),
        out_specs=ANY,
        scratch_shapes=[
            pltpu.VMEM((nb // LANES, n * nz, LANES), F32),
            pltpu.VMEM((n, nb), F32),
            pltpu.VMEM((parts, n // ny // parts, ny, nz, nb), BF16),
            pltpu.SemaphoreType.DMA((parts,)),
        ],
        input_output_aliases={} if prev is None else {6: 0},
        compiler_params=pltpu.CompilerParams(vmem_limit_bytes=16 * MIB),
        name="finish",
    )(*given)


def inner(spectrum, we, wn):
    nx, ny, nz, nb = spectrum.shape
    return pl.pallas_call(
        inner_kernel,
        out_shape=pltpu.VMEM((nb // LANES, nx * ny * nz, LANES), F32),
        in_specs=[HBM] * 3,
        out_specs=VMEM,
        scratch_shapes=[
            pltpu.VMEM(spectrum.shape, BF16),
            pltpu.VMEM(we.shape, F32),
            pltpu.VMEM(wn.shape, F32),
            pltpu.SemaphoreType.DMA((5,)),
        ],
        compiler_params=pltpu.CompilerParams(vmem_limit_bytes=8 * MIB),
        cost_estimate=pl.CostEstimate(flops=10**7, bytes_accessed=16 * MIB, transcendentals=0),
        name="inner",
    )(in_hbm(spectrum), in_hbm(we), in_hbm(wn))


def cloud(place, cells, target, adv, halo, we, wn, fall, pi, po, lk, fr, count):
    blk, blocks = cells.shape
    nb = fall.shape[1]
    return pl.pallas_call(
        cloud_kernel,
        out_shape=(
            pltpu.VMEM(adv.shape, F32),
            pltpu.VMEM((count + GAIN_ROWS, nb), BF16),
        ),
        in_specs=[SMEM, ANY, ANY] + [VMEM] * 12,
        out_specs=(VMEM, VMEM),
        scratch_shapes=[
            pltpu.SMEM((blk, blocks), jnp.int32),
            pltpu.SMEM((1, blocks), jnp.int32),
            pltpu.VMEM((nb // LANES, blk * blocks, LANES), F32),
            pltpu.SemaphoreType.DMA((2,)),
        ],
        input_output_aliases={3: 0},
        compiler_params=pltpu.CompilerParams(vmem_limit_bytes=16 * MIB),
        name="cloud",
    )(place, cells, target, in_vmem(adv), *halo, we, wn, fall, pi, po, lk, fr)


def settle(adv, fall, count):
    nb = fall.shape[1]
    return pl.pallas_call(
        settle_kernel,
        out_shape=(
            pltpu.HBM(adv.shape, F32),
            pltpu.VMEM((count + GAIN_ROWS, nb), BF16),
        ),
        in_specs=[VMEM, VMEM],
        out_specs=(HBM, VMEM),
        scratch_shapes=[pltpu.SemaphoreType.DMA((2,))],
        compiler_params=pltpu.CompilerParams(vmem_limit_bytes=4 * MIB),
        name="settle",
    )(in_vmem(adv), fall)


def body(
    spectrum,
    wind_east,
    wind_north,
    fall_rate,
    cloud_cells,
    block_target,
    pair_inputs,
    pair_outputs,
    loss_kernel,
    fragments,
):
    nx, ny, nz, nb = spectrum.shape
    n_gx, n_gy = (lax.axis_size(a) for a in ("gx", "gy"))
    up_x = [(i, (i + 1) % n_gx) for i in range(n_gx)]
    up_y = [(i, (i + 1) % n_gy) for i in range(n_gy)]
    low_x, high_x, low_y, high_y = edges(spectrum)
    south = lax.ppermute(high_y, "gy", up_y)
    north = lax.ppermute(low_y, "gy", [(b, a) for a, b in up_y])
    west = lax.ppermute(high_x, "gx", up_x)
    east = lax.ppermute(low_x, "gx", [(b, a) for a, b in up_x])

    we, wn = wind_east.transpose(0, 2, 1), wind_north.transpose(0, 2, 1)
    adv = inner(spectrum, we, wn)
    blocks, blk = cloud_cells.shape[3:]
    cells = cloud_cells.reshape(blocks, blk).T
    place = jnp.stack([lax.axis_index("gx"), lax.axis_index("gy")])
    zid = lax.axis_index("gz").reshape(1)
    columns = nx * ny
    first = columns // 2
    adv, flux = cloud(
        place,
        cells,
        block_target,
        adv,
        (west, east, south, north),
        we,
        wn,
        fall_rate,
        pair_inputs,
        pair_outputs,
        loss_kernel,
        fragments,
        first,
    )

    def begin(flux):
        a = lax.ppermute(flux, "gz", [(3, 2), (2, 1)])
        b = lax.ppermute(flux, "gz", [(3, 0)])
        return flux, a, b

    front = begin(flux)
    local, flux = settle(adv, fall_rate, columns - first)
    back = begin(flux)
    ready = []
    for flux, a, b in (front, back):
        ready.append((a, b, lax.ppermute(combine(zid, flux, a, b), "gz", [(1, 0), (0, 1)])))
    front, back = ready
    shape = spectrum.shape
    out = finish(zid, fall_rate, *front, local, None, shape, 0, 4)
    out = finish(zid, fall_rate, *back, local, out, shape, first // ny, 4)
    return out


def solution(mesh):
    in_specs = (
        P("gx", "gy", "gz", None),
        P("gx", "gy", "gz"),
        P("gx", "gy", "gz"),
        P("gz", None),
        P("gx", "gy", "gz", None, None),
        P(None, None, "gz", None),
        P(),
        P(),
        P(),
        P(),
    )
    out_specs = P("gx", "gy", "gz", None)
    return jax.shard_map(body, mesh=mesh, in_specs=in_specs, out_specs=out_specs, check_vma=False)
```

```python
import functools

import jax
import jax.numpy as jnp
from jax import lax
from jax.experimental import pallas as pl
from jax.experimental.pallas import tpu as pltpu
from jax.sharding import PartitionSpec as P

F32 = jnp.float32
BF16 = jnp.bfloat16
LANES = 128
GROUP = 4
GAIN_ROWS = 16
MIB = 2**20
VMEM = pl.BlockSpec(memory_space=pltpu.VMEM)
SMEM = pl.BlockSpec(memory_space=pltpu.SMEM)
ANY = pl.BlockSpec(memory_space=pl.ANY)
HBM = pl.BlockSpec(memory_space=pltpu.HBM)
in_hbm = functools.partial(pltpu.with_memory_space_constraint, memory_space=pltpu.HBM)
in_vmem = functools.partial(pltpu.with_memory_space_constraint, memory_space=pltpu.VMEM)


def edges_kernel(s_ref, west_ref, east_ref, south_ref, north_ref, sems):
    nx, ny = s_ref.shape[:2]
    pieces = (
        (s_ref.at[0:1], west_ref),
        (s_ref.at[nx - 1 : nx], east_ref),
        (s_ref.at[:, 0:1], south_ref),
        (s_ref.at[:, ny - 1 : ny], north_ref),
    )
    copies = [
        pltpu.make_async_copy(src, dst, sems.at[i]) for i, (src, dst) in enumerate(pieces)
    ]
    for copy in copies:
        copy.start()
    for copy in copies:
        copy.wait()


def edges(spectrum):
    nx, ny, nz, nb = spectrum.shape
    row = jax.ShapeDtypeStruct((1, ny, nz, nb), BF16)
    column = jax.ShapeDtypeStruct((nx, 1, nz, nb), BF16)
    return pl.pallas_call(
        edges_kernel,
        out_shape=(row, row, column, column),
        in_specs=[HBM],
        out_specs=[ANY] * 4,
        scratch_shapes=[pltpu.SemaphoreType.DMA((4,))],
        compiler_params=pltpu.CompilerParams(vmem_limit_bytes=MIB),
        name="edges",
    )(in_hbm(spectrum))


def wide(c, y, shape):
    return jnp.broadcast_to(c[:, y : y + 1], shape)


def inner_kernel(s_any, we_any, wn_any, adv, s_ref, we_ref, wn_ref, sems):
    nx, ny, nz, nb = s_ref.shape
    winds = [
        pltpu.make_async_copy(we_any, we_ref, sems.at[0]),
        pltpu.make_async_copy(wn_any, wn_ref, sems.at[1]),
    ]
    cuts = (0, GROUP + 1, nx // 2 + 1, nx)
    loads = [
        pltpu.make_async_copy(s_any.at[lo:hi], s_ref.at[lo:hi], sems.at[2 + i])
        for i, (lo, hi) in enumerate(zip(cuts, cuts[1:]))
    ]
    for copy in winds + loads:
        copy.start()
    for copy in winds:
        copy.wait()

    half = (nz, LANES)
    none = jnp.zeros((nz, nb), F32)

    def advect(g, carry):
        x = g * GROUP
        before, after = jnp.maximum(x - 1, 0), jnp.minimum(x + GROUP, nx - 1)
        has_before = jnp.where(x > 0, 1.0, 0.0)
        has_after = jnp.where(x + GROUP < nx, 1.0, 0.0)
        us = [we_ref[x + r] for r in range(GROUP)]
        vs = [wn_ref[x + r] for r in range(GROUP)]
        behind = [none] * GROUP
        here = [s_ref[x + r, 0].astype(F32) for r in range(GROUP)]
        for y in range(ny):
            if y < ny - 1:
                ahead = [s_ref[x + r, y + 1].astype(F32) for r in range(GROUP)]
            else:
                ahead = [none] * GROUP
            line = [
                s_ref[before, y].astype(F32) * has_before,
                *here,
                s_ref[after, y].astype(F32) * has_after,
            ]
            for r in range(GROUP):
                u, v = wide(us[r], y, half), wide(vs[r], y, half)
                from_low, from_south = u > 0.0, v > 0.0
                u, v = jnp.abs(u), jnp.abs(v)
                at = pl.ds(pl.multiple_of(((x + r) * ny + y) * nz, 8), nz)
                for t in range(nb // LANES):
                    lanes = slice(t * LANES, (t + 1) * LANES)
                    own = here[r][:, lanes]
                    side = jnp.where(from_low, line[r][:, lanes], line[r + 2][:, lanes])
                    other = jnp.where(from_south, behind[r][:, lanes], ahead[r][:, lanes])
                    adv[t, at, :] = own + u * (side - own) + v * (other - own)
            behind, here = here, ahead
        return carry

    done = 0
    for hi, copy in zip(cuts[1:], loads):
        copy.wait()
        ready = (nx if hi == nx else hi - 1) // GROUP
        lax.fori_loop(done, ready, advect, 0)
        done = ready


def settle_columns(adv, flux_ref, fall, first, count):
    nz, nb = fall.shape
    inverse = 1.0 / (1.0 + fall)
    through = fall * inverse
    tiles = adv.shape[0]

    def settle(g, carry):
        base = pl.multiple_of((first + g * 16) * nz, 128)
        for t in range(tiles):
            lanes = slice(t * LANES, (t + 1) * LANES)
            flows = []
            for half in range(2):
                inflow = jnp.zeros((8, LANES), F32)
                for z in reversed(range(nz)):
                    at = pl.ds(base + half * 8 * nz + z, 8, stride=nz)
                    total = adv[t, at, :] + inflow
                    adv[t, at, :] = total * inverse[z : z + 1, lanes]
                    inflow = total * through[z : z + 1, lanes]
                flows.append(inflow)
            flux_ref[pl.ds(pl.multiple_of(g * 16, 16), 16), lanes] = jnp.concatenate(
                flows, 0
            ).astype(BF16)
        return carry

    lax.fori_loop(0, count // 16, settle, 0, unroll=2)
    gain = jnp.ones((1, nb), F32)
    for z in reversed(range(nz)):
        gain = gain * through[z : z + 1, :]
    flux_ref[pl.ds(count, GAIN_ROWS), :] = jnp.broadcast_to(gain, (GAIN_ROWS, nb)).astype(BF16)


def cloud_kernel(
    place_ref,
    cells_any,
    target_any,
    adv_in,
    west_ref,
    east_ref,
    south_ref,
    north_ref,
    we_ref,
    wn_ref,
    fall_ref,
    pi_ref,
    po_ref,
    lk_ref,
    fr_ref,
    adv,
    flux_ref,
    cells,
    target,
    rows,
    sems,
):
    del adv_in
    nx, nz, ny = we_ref.shape
    nb = fall_ref.shape[1]
    blk, blocks = cells.shape
    pairs = po_ref.shape[0]
    tiles = nb // LANES
    plane = target_any.shape[0] * target_any.shape[1]
    lists = pltpu.make_async_copy(cells_any, cells, sems.at[0])
    routes = pltpu.make_async_copy(target_any.at[place_ref[0], place_ref[1]], target, sems.at[1])
    lists.start()
    routes.start()

    def add(cell, value):
        at = pl.ds(pl.multiple_of(cell, 8), nz)
        for t in range(tiles):
            adv[t, at, :] += value[:, t * LANES : (t + 1) * LANES]

    shape = (nz, nb)
    c_w = jnp.maximum(we_ref[0], 0.0)
    c_e = jnp.maximum(-we_ref[nx - 1], 0.0)
    for y in range(ny):
        add(y * nz, wide(c_w, y, shape) * west_ref[0, y].astype(F32))
        add(((nx - 1) * ny + y) * nz, wide(c_e, y, shape) * east_ref[0, y].astype(F32))

    def sides(i, carry):
        for k in range(4):
            x = i * 4 + k
            v = wn_ref[x]
            c_s = jnp.maximum(v, 0.0)
            c_n = jnp.maximum(-v, 0.0)
            add(x * ny * nz, wide(c_s, 0, shape) * south_ref[x, 0].astype(F32))
            add((x * ny + ny - 1) * nz, wide(c_n, ny - 1, shape) * north_ref[x, 0].astype(F32))
        return carry

    lax.fori_loop(0, nx // 4, sides, 0)
    lists.wait()

    def gather(b, carry):
        base = pl.multiple_of(b * blk, blk)
        for j in range(blk):
            for t in range(tiles):
                rows[t, pl.ds(base + j, 1), :] = adv[t, pl.ds(cells[j, b], 1), :]
        return carry

    lax.fori_loop(0, blocks, gather, 0, unroll=2)

    step = 1024
    tile = 512

    def collide(i, carry):
        here = pl.ds(pl.multiple_of(i * step, step), step)
        cloud = jnp.concatenate([rows[t, here, :] for t in range(tiles)], 1).astype(BF16)
        decline = jnp.dot(cloud, lk_ref[...], preferred_element_type=F32)
        losses = cloud.astype(F32) * decline
        total = jnp.dot(losses.astype(BF16), fr_ref[...], preferred_element_type=F32) - losses
        for n in range(pairs // tile):
            left = jnp.dot(
                cloud, pi_ref[:, n * tile : (n + 1) * tile], preferred_element_type=F32
            )
            right = jnp.dot(
                cloud,
                pi_ref[:, pairs + n * tile : pairs + (n + 1) * tile],
                preferred_element_type=F32,
            )
            total = total + jnp.dot(
                (left * right).astype(BF16),
                po_ref[n * tile : (n + 1) * tile, :],
                preferred_element_type=F32,
            )
        total = total.astype(BF16).astype(F32)
        for t in range(tiles):
            rows[t, here, :] += total[:, t * LANES : (t + 1) * LANES]
        return carry

    lax.fori_loop(0, blocks * blk // step, collide, 0)
    routes.wait()

    def scatter(b, carry):
        base = pl.multiple_of(b * blk, blk)

        @pl.when(target[0, b] < plane)
        def _():
            for j in range(blk):
                for t in range(tiles):
                    adv[t, pl.ds(cells[j, b], 1), :] = rows[t, pl.ds(base + j, 1), :]

        return carry

    lax.fori_loop(0, blocks, scatter, 0, unroll=4)
    count = flux_ref.shape[0] - GAIN_ROWS
    settle_columns(adv, flux_ref, fall_ref[...], 0, count)


def settle_kernel(adv, fall_ref, local_any, flux_ref, sems):
    nz = fall_ref.shape[0]
    count = flux_ref.shape[0] - GAIN_ROWS
    first = adv.shape[1] // nz - count
    cut = first * nz
    front = pltpu.make_async_copy(adv.at[:, :cut], local_any.at[:, :cut], sems.at[0])
    back = pltpu.make_async_copy(adv.at[:, cut:], local_any.at[:, cut:], sems.at[1])
    front.start()
    settle_columns(adv, flux_ref, fall_ref[...], first, count)
    back.start()
    front.wait()
    back.wait()


def combine_kernel(zid_ref, own_ref, a_ref, b_ref, out_ref):
    n = own_ref.shape[0] - GAIN_ROWS
    z = zid_ref[0]

    @pl.when(z == 0)
    def _():
        out_ref[...] = b_ref[...]

    @pl.when(z != 0)
    def _():
        gain = own_ref[n : n + GAIN_ROWS, :].astype(F32)

        def some(i, carry):
            at = pl.ds(pl.multiple_of(i * 16, 16), 16)
            out_ref[at, :] = (
                own_ref[at, :].astype(F32) + gain * a_ref[at, :].astype(F32)
            ).astype(BF16)
            return carry

        lax.fori_loop(0, n // 16, some, 0, unroll=4)
        out_ref[n : n + GAIN_ROWS, :] = (
            gain * a_ref[n : n + GAIN_ROWS, :].astype(F32)
        ).astype(BF16)


def combine(zid, own, a, b):
    return pl.pallas_call(
        combine_kernel,
        out_shape=pltpu.VMEM(own.shape, BF16),
        in_specs=[SMEM] + [VMEM] * 3,
        out_specs=VMEM,
        compiler_params=pltpu.CompilerParams(vmem_limit_bytes=4 * MIB),
        name="combine",
    )(zid, own, a, b)


def finish_kernel(
    zid_ref,
    fall_ref,
    a_ref,
    b_ref,
    d_ref,
    local_any,
    prev_ref,
    out_any,
    local,
    inflow,
    stage,
    sems,
    *,
    first,
):
    del prev_ref
    ny, nz, nb = out_any.shape[1:]
    parts, per = stage.shape[:2]
    tiles = nb // LANES
    n = a_ref.shape[0] - GAIN_ROWS
    span = per * ny * nz
    loads = []
    for p in range(parts):
        start = first * ny * nz + p * span
        loads.append(
            pltpu.make_async_copy(
                local_any.at[:, start : start + span],
                local.at[:, p * span : (p + 1) * span],
                sems.at[p],
            )
        )
        loads[-1].start()
    fall = fall_ref[...]
    inverse = 1.0 / (1.0 + fall)
    through = fall * inverse
    carried = jnp.ones((1, nb), F32)
    gains = [None] * nz
    for level in reversed(range(nz)):
        gains[level] = carried * inverse[level : level + 1, :]
        carried = carried * through[level : level + 1, :]
    gain = jnp.concatenate(gains, 0)
    bottom = zid_ref[0] == 0
    mix = jnp.where(bottom, d_ref[n : n + GAIN_ROWS, :], a_ref[n : n + GAIN_ROWS, :]).astype(F32)

    def enter(i, carry):
        at = pl.ds(pl.multiple_of(i * 16, 16), 16)
        a, b, d = a_ref[at, :].astype(F32), b_ref[at, :].astype(F32), d_ref[at, :].astype(F32)
        inflow[at, :] = jnp.where(bottom, d, a) + mix * jnp.where(bottom, b, d)
        return carry

    lax.fori_loop(0, n // 16, enter, 0, unroll=4)
    copies = []
    for p in range(parts):

        def column(x, carry, p=p):
            base = (p * per + x) * ny
            for y in range(ny):
                at = pl.ds(pl.multiple_of((base + y) * nz, 8), nz)
                m = jnp.broadcast_to(inflow[pl.ds(base + y, 1), :], (nz, nb))
                own = jnp.concatenate([local[t, at, :] for t in range(tiles)], 1)
                stage[p, x, y] = (own + m * gain).astype(BF16)
            return carry

        loads[p].wait()
        lax.fori_loop(0, per, column, 0)
        copy = pltpu.make_async_copy(
            stage.at[p], out_any.at[first + p * per : first + (p + 1) * per], sems.at[p]
        )
        copy.start()
        copies.append(copy)
    for copy in copies:
        copy.wait()


def finish(zid, fall, a, b, d, local, prev, shape, first, parts):
    nx, ny, nz, nb = shape
    n = a.shape[0] - GAIN_ROWS
    given = (zid, fall, a, b, d, in_hbm(local)) + (() if prev is None else (prev,))
    kernel = functools.partial(finish_kernel, first=first)
    if prev is None:
        inner = kernel

        def kernel(*refs):
            return inner(*refs[:6], None, *refs[6:])

    return pl.pallas_call(
        kernel,
        out_shape=jax.ShapeDtypeStruct(shape, BF16),
        in_specs=[SMEM] + [VMEM] * 4 + [HBM] + [ANY] * (prev is not None),
        out_specs=ANY,
        scratch_shapes=[
            pltpu.VMEM((nb // LANES, n * nz, LANES), F32),
            pltpu.VMEM((n, nb), F32),
            pltpu.VMEM((parts, n // ny // parts, ny, nz, nb), BF16),
            pltpu.SemaphoreType.DMA((parts,)),
        ],
        input_output_aliases={} if prev is None else {6: 0},
        compiler_params=pltpu.CompilerParams(vmem_limit_bytes=16 * MIB),
        name="finish",
    )(*given)


def inner(spectrum, we, wn):
    nx, ny, nz, nb = spectrum.shape
    return pl.pallas_call(
        inner_kernel,
        out_shape=pltpu.VMEM((nb // LANES, nx * ny * nz, LANES), F32),
        in_specs=[HBM] * 3,
        out_specs=VMEM,
        scratch_shapes=[
            pltpu.VMEM(spectrum.shape, BF16),
            pltpu.VMEM(we.shape, F32),
            pltpu.VMEM(wn.shape, F32),
            pltpu.SemaphoreType.DMA((5,)),
        ],
        compiler_params=pltpu.CompilerParams(vmem_limit_bytes=8 * MIB),
        cost_estimate=pl.CostEstimate(flops=10**7, bytes_accessed=16 * MIB, transcendentals=0),
        name="inner",
    )(in_hbm(spectrum), in_hbm(we), in_hbm(wn))


def cloud(place, cells, target, adv, halo, we, wn, fall, pi, po, lk, fr, count):
    blk, blocks = cells.shape
    nb = fall.shape[1]
    return pl.pallas_call(
        cloud_kernel,
        out_shape=(
            pltpu.VMEM(adv.shape, F32),
            pltpu.VMEM((count + GAIN_ROWS, nb), BF16),
        ),
        in_specs=[SMEM, ANY, ANY] + [VMEM] * 12,
        out_specs=(VMEM, VMEM),
        scratch_shapes=[
            pltpu.SMEM((blk, blocks), jnp.int32),
            pltpu.SMEM((1, blocks), jnp.int32),
            pltpu.VMEM((nb // LANES, blk * blocks, LANES), F32),
            pltpu.SemaphoreType.DMA((2,)),
        ],
        input_output_aliases={3: 0},
        compiler_params=pltpu.CompilerParams(vmem_limit_bytes=16 * MIB),
        name="cloud",
    )(place, cells, target, in_vmem(adv), *halo, we, wn, fall, pi, po, lk, fr)


def settle(adv, fall, count):
    nb = fall.shape[1]
    return pl.pallas_call(
        settle_kernel,
        out_shape=(
            pltpu.HBM(adv.shape, F32),
            pltpu.VMEM((count + GAIN_ROWS, nb), BF16),
        ),
        in_specs=[VMEM, VMEM],
        out_specs=(HBM, VMEM),
        scratch_shapes=[pltpu.SemaphoreType.DMA((2,))],
        compiler_params=pltpu.CompilerParams(vmem_limit_bytes=4 * MIB),
        name="settle",
    )(in_vmem(adv), fall)


def body(
    spectrum,
    wind_east,
    wind_north,
    fall_rate,
    cloud_cells,
    block_target,
    pair_inputs,
    pair_outputs,
    loss_kernel,
    fragments,
):
    nx, ny, nz, nb = spectrum.shape
    n_gx, n_gy = (lax.axis_size(a) for a in ("gx", "gy"))
    up_x = [(i, (i + 1) % n_gx) for i in range(n_gx)]
    up_y = [(i, (i + 1) % n_gy) for i in range(n_gy)]
    low_x, high_x, low_y, high_y = edges(spectrum)
    south = lax.ppermute(high_y, "gy", up_y)
    north = lax.ppermute(low_y, "gy", [(b, a) for a, b in up_y])
    west = lax.ppermute(high_x, "gx", up_x)
    east = lax.ppermute(low_x, "gx", [(b, a) for a, b in up_x])

    we, wn = wind_east.transpose(0, 2, 1), wind_north.transpose(0, 2, 1)
    adv = inner(spectrum, we, wn)
    blocks, blk = cloud_cells.shape[3:]
    cells = cloud_cells.reshape(blocks, blk).T
    place = jnp.stack([lax.axis_index("gx"), lax.axis_index("gy")])
    zid = lax.axis_index("gz").reshape(1)
    columns = nx * ny
    first = 16 * ny
    adv, flux = cloud(
        place,
        cells,
        block_target,
        adv,
        (west, east, south, north),
        we,
        wn,
        fall_rate,
        pair_inputs,
        pair_outputs,
        loss_kernel,
        fragments,
        first,
    )

    def begin(flux):
        a = lax.ppermute(flux, "gz", [(3, 2), (2, 1)])
        b = lax.ppermute(flux, "gz", [(3, 0)])
        return flux, a, b

    front = begin(flux)
    local, flux = settle(adv, fall_rate, columns - first)
    back = begin(flux)
    ready = []
    for flux, a, b in (front, back):
        ready.append((a, b, lax.ppermute(combine(zid, flux, a, b), "gz", [(1, 0), (0, 1)])))
    front, back = ready
    shape = spectrum.shape
    out = finish(zid, fall_rate, *front, local, None, shape, 0, 4)
    out = finish(zid, fall_rate, *back, local, out, shape, first // ny, 4)
    return out


def solution(mesh):
    in_specs = (
        P("gx", "gy", "gz", None),
        P("gx", "gy", "gz"),
        P("gx", "gy", "gz"),
        P("gz", None),
        P("gx", "gy", "gz", None, None),
        P(None, None, "gz", None),
        P(),
        P(),
        P(),
        P(),
    )
    out_specs = P("gx", "gy", "gz", None)
    return jax.shard_map(body, mesh=mesh, in_specs=in_specs, out_specs=out_specs, check_vma=False)
```

```python
import functools

import jax
import jax.numpy as jnp
from jax import lax
from jax.experimental import pallas as pl
from jax.experimental.pallas import tpu as pltpu
from jax.sharding import PartitionSpec as P

F32 = jnp.float32
BF16 = jnp.bfloat16
LANES = 128
GROUP = 4
GAIN_ROWS = 16
MIB = 2**20
VMEM = pl.BlockSpec(memory_space=pltpu.VMEM)
SMEM = pl.BlockSpec(memory_space=pltpu.SMEM)
ANY = pl.BlockSpec(memory_space=pl.ANY)
HBM = pl.BlockSpec(memory_space=pltpu.HBM)
in_hbm = functools.partial(pltpu.with_memory_space_constraint, memory_space=pltpu.HBM)
in_vmem = functools.partial(pltpu.with_memory_space_constraint, memory_space=pltpu.VMEM)


def edges_kernel(s_ref, west_ref, east_ref, south_ref, north_ref, sems):
    nx, ny = s_ref.shape[:2]
    pieces = (
        (s_ref.at[0:1], west_ref),
        (s_ref.at[nx - 1 : nx], east_ref),
        (s_ref.at[:, 0:1], south_ref),
        (s_ref.at[:, ny - 1 : ny], north_ref),
    )
    copies = [
        pltpu.make_async_copy(src, dst, sems.at[i]) for i, (src, dst) in enumerate(pieces)
    ]
    for copy in copies:
        copy.start()
    for copy in copies:
        copy.wait()


def edges(spectrum):
    nx, ny, nz, nb = spectrum.shape
    row = jax.ShapeDtypeStruct((1, ny, nz, nb), BF16)
    column = jax.ShapeDtypeStruct((nx, 1, nz, nb), BF16)
    return pl.pallas_call(
        edges_kernel,
        out_shape=(row, row, column, column),
        in_specs=[HBM],
        out_specs=[ANY] * 4,
        scratch_shapes=[pltpu.SemaphoreType.DMA((4,))],
        compiler_params=pltpu.CompilerParams(vmem_limit_bytes=MIB),
        name="edges",
    )(in_hbm(spectrum))


def wide(c, y, shape):
    return jnp.broadcast_to(c[:, y : y + 1], shape)


def inner_kernel(s_any, we_any, wn_any, adv, s_ref, we_ref, wn_ref, sems):
    nx, ny, nz, nb = s_ref.shape
    winds = [
        pltpu.make_async_copy(we_any, we_ref, sems.at[0]),
        pltpu.make_async_copy(wn_any, wn_ref, sems.at[1]),
    ]
    cuts = (0, GROUP + 1, nx // 2 + 1, nx)
    loads = [
        pltpu.make_async_copy(s_any.at[lo:hi], s_ref.at[lo:hi], sems.at[2 + i])
        for i, (lo, hi) in enumerate(zip(cuts, cuts[1:]))
    ]
    for copy in winds + loads:
        copy.start()
    for copy in winds:
        copy.wait()

    half = (nz, LANES)
    none = jnp.zeros((nz, nb), F32)

    def advect(g, carry):
        x = g * GROUP
        before, after = jnp.maximum(x - 1, 0), jnp.minimum(x + GROUP, nx - 1)
        has_before = jnp.where(x > 0, 1.0, 0.0)
        has_after = jnp.where(x + GROUP < nx, 1.0, 0.0)
        us = [we_ref[x + r] for r in range(GROUP)]
        vs = [wn_ref[x + r] for r in range(GROUP)]
        behind = [none] * GROUP
        here = [s_ref[x + r, 0].astype(F32) for r in range(GROUP)]
        for y in range(ny):
            if y < ny - 1:
                ahead = [s_ref[x + r, y + 1].astype(F32) for r in range(GROUP)]
            else:
                ahead = [none] * GROUP
            line = [
                s_ref[before, y].astype(F32) * has_before,
                *here,
                s_ref[after, y].astype(F32) * has_after,
            ]
            for r in range(GROUP):
                u, v = wide(us[r], y, half), wide(vs[r], y, half)
                from_low, from_south = u > 0.0, v > 0.0
                u, v = jnp.abs(u), jnp.abs(v)
                at = pl.ds(pl.multiple_of(((x + r) * ny + y) * nz, 8), nz)
                for t in range(nb // LANES):
                    lanes = slice(t * LANES, (t + 1) * LANES)
                    own = here[r][:, lanes]
                    side = jnp.where(from_low, line[r][:, lanes], line[r + 2][:, lanes])
                    other = jnp.where(from_south, behind[r][:, lanes], ahead[r][:, lanes])
                    adv[t, at, :] = own + u * (side - own) + v * (other - own)
            behind, here = here, ahead
        return carry

    done = 0
    for hi, copy in zip(cuts[1:], loads):
        copy.wait()
        ready = (nx if hi == nx else hi - 1) // GROUP
        lax.fori_loop(done, ready, advect, 0)
        done = ready


def settle_columns(adv, flux_ref, fall, first, count):
    nz, nb = fall.shape
    inverse = 1.0 / (1.0 + fall)
    through = fall * inverse
    tiles = adv.shape[0]

    def settle(g, carry):
        base = pl.multiple_of((first + g * 16) * nz, 128)
        for t in range(tiles):
            lanes = slice(t * LANES, (t + 1) * LANES)
            flows = []
            for half in range(2):
                inflow = jnp.zeros((8, LANES), F32)
                for z in reversed(range(nz)):
                    at = pl.ds(base + half * 8 * nz + z, 8, stride=nz)
                    total = adv[t, at, :] + inflow
                    adv[t, at, :] = total * inverse[z : z + 1, lanes]
                    inflow = total * through[z : z + 1, lanes]
                flows.append(inflow)
            flux_ref[pl.ds(pl.multiple_of(g * 16, 16), 16), lanes] = jnp.concatenate(
                flows, 0
            ).astype(BF16)
        return carry

    lax.fori_loop(0, count // 16, settle, 0, unroll=2)
    gain = jnp.ones((1, nb), F32)
    for z in reversed(range(nz)):
        gain = gain * through[z : z + 1, :]
    rest = flux_ref.shape[0] - count
    flux_ref[pl.ds(count, rest), :] = jnp.broadcast_to(gain, (rest, nb)).astype(BF16)


def cloud_kernel(
    place_ref,
    cells_any,
    target_any,
    adv_in,
    west_ref,
    east_ref,
    south_ref,
    north_ref,
    we_ref,
    wn_ref,
    fall_ref,
    pi_ref,
    po_ref,
    lk_ref,
    fr_ref,
    adv,
    flux_ref,
    cells,
    target,
    rows,
    sems,
):
    del adv_in
    nx, nz, ny = we_ref.shape
    nb = fall_ref.shape[1]
    blk, blocks = cells.shape
    pairs = po_ref.shape[0]
    tiles = nb // LANES
    plane = target_any.shape[0] * target_any.shape[1]
    lists = pltpu.make_async_copy(cells_any, cells, sems.at[0])
    routes = pltpu.make_async_copy(target_any.at[place_ref[0], place_ref[1]], target, sems.at[1])
    lists.start()
    routes.start()

    def add(cell, value):
        at = pl.ds(pl.multiple_of(cell, 8), nz)
        for t in range(tiles):
            adv[t, at, :] += value[:, t * LANES : (t + 1) * LANES]

    shape = (nz, nb)
    c_w = jnp.maximum(we_ref[0], 0.0)
    c_e = jnp.maximum(-we_ref[nx - 1], 0.0)
    for y in range(ny):
        add(y * nz, wide(c_w, y, shape) * west_ref[0, y].astype(F32))
        add(((nx - 1) * ny + y) * nz, wide(c_e, y, shape) * east_ref[0, y].astype(F32))

    def sides(i, carry):
        for k in range(4):
            x = i * 4 + k
            v = wn_ref[x]
            c_s = jnp.maximum(v, 0.0)
            c_n = jnp.maximum(-v, 0.0)
            add(x * ny * nz, wide(c_s, 0, shape) * south_ref[x, 0].astype(F32))
            add((x * ny + ny - 1) * nz, wide(c_n, ny - 1, shape) * north_ref[x, 0].astype(F32))
        return carry

    lax.fori_loop(0, nx // 4, sides, 0)
    lists.wait()

    def gather(b, carry):
        base = pl.multiple_of(b * blk, blk)
        for j in range(blk):
            for t in range(tiles):
                rows[t, pl.ds(base + j, 1), :] = adv[t, pl.ds(cells[j, b], 1), :]
        return carry

    lax.fori_loop(0, blocks, gather, 0, unroll=2)

    step = 1024
    tile = 512

    def collide(i, carry):
        here = pl.ds(pl.multiple_of(i * step, step), step)
        cloud = jnp.concatenate([rows[t, here, :] for t in range(tiles)], 1).astype(BF16)
        decline = jnp.dot(cloud, lk_ref[...], preferred_element_type=F32)
        losses = cloud.astype(F32) * decline
        total = jnp.dot(losses.astype(BF16), fr_ref[...], preferred_element_type=F32) - losses
        for n in range(pairs // tile):
            left = jnp.dot(
                cloud, pi_ref[:, n * tile : (n + 1) * tile], preferred_element_type=F32
            )
            right = jnp.dot(
                cloud,
                pi_ref[:, pairs + n * tile : pairs + (n + 1) * tile],
                preferred_element_type=F32,
            )
            total = total + jnp.dot(
                (left * right).astype(BF16),
                po_ref[n * tile : (n + 1) * tile, :],
                preferred_element_type=F32,
            )
        total = total.astype(BF16).astype(F32)
        for t in range(tiles):
            rows[t, here, :] += total[:, t * LANES : (t + 1) * LANES]
        return carry

    lax.fori_loop(0, blocks * blk // step, collide, 0)
    routes.wait()

    def scatter(b, carry):
        base = pl.multiple_of(b * blk, blk)

        @pl.when(target[0, b] < plane)
        def _():
            for j in range(blk):
                for t in range(tiles):
                    adv[t, pl.ds(cells[j, b], 1), :] = rows[t, pl.ds(base + j, 1), :]

        return carry

    lax.fori_loop(0, blocks, scatter, 0, unroll=4)
    count = flux_ref.shape[0] - 4 * GAIN_ROWS
    settle_columns(adv, flux_ref, fall_ref[...], 0, count)


def settle_kernel(adv, fall_ref, local_any, flux_ref, sems):
    nz = fall_ref.shape[0]
    count = flux_ref.shape[0] - 2 * GAIN_ROWS
    first = adv.shape[1] // nz - count
    cut = first * nz
    front = pltpu.make_async_copy(adv.at[:, :cut], local_any.at[:, :cut], sems.at[0])
    back = pltpu.make_async_copy(adv.at[:, cut:], local_any.at[:, cut:], sems.at[1])
    front.start()
    settle_columns(adv, flux_ref, fall_ref[...], first, count)
    back.start()
    front.wait()
    back.wait()


def combine_kernel(zid_ref, own_ref, a_ref, b_ref, out_ref, *, n):
    z = zid_ref[0]

    @pl.when(z == 0)
    def _():
        out_ref[...] = b_ref[0 : own_ref.shape[0], :]

    @pl.when(z != 0)
    def _():
        gain = own_ref[n : n + GAIN_ROWS, :].astype(F32)

        def some(i, carry):
            at = pl.ds(pl.multiple_of(i * 16, 16), 16)
            out_ref[at, :] = (
                own_ref[at, :].astype(F32) + gain * a_ref[at, :].astype(F32)
            ).astype(BF16)
            return carry

        lax.fori_loop(0, n // 16, some, 0, unroll=4)
        for row in range(n, own_ref.shape[0], GAIN_ROWS):
            at = slice(row, row + GAIN_ROWS)
            out_ref[at, :] = (gain * a_ref[at, :].astype(F32)).astype(BF16)


def combine(zid, own, a, b, n):
    return pl.pallas_call(
        functools.partial(combine_kernel, n=n),
        out_shape=pltpu.VMEM(own.shape, BF16),
        in_specs=[SMEM] + [VMEM] * 3,
        out_specs=VMEM,
        compiler_params=pltpu.CompilerParams(vmem_limit_bytes=4 * MIB),
        name="combine",
    )(zid, own, a, b)


def finish_columns(
    zid_ref, fall_ref, a_ref, b_ref, d_ref, out_any, local, inflow, stage, sems, first, loads, later
):
    ny, nz, nb = out_any.shape[1:]
    parts, per = stage.shape[:2]
    tiles = nb // LANES
    n = inflow.shape[0]
    fall = fall_ref[...]
    inverse = 1.0 / (1.0 + fall)
    through = fall * inverse
    carried = jnp.ones((1, nb), F32)
    gains = [None] * nz
    for level in reversed(range(nz)):
        gains[level] = carried * inverse[level : level + 1, :]
        carried = carried * through[level : level + 1, :]
    gain = jnp.concatenate(gains, 0)
    bottom = zid_ref[0] == 0
    mix = jnp.where(bottom, d_ref[n : n + GAIN_ROWS, :], a_ref[n : n + GAIN_ROWS, :]).astype(F32)

    def enter(i, carry):
        at = pl.ds(pl.multiple_of(i * 16, 16), 16)
        a, b, d = a_ref[at, :].astype(F32), b_ref[at, :].astype(F32), d_ref[at, :].astype(F32)
        inflow[at, :] = jnp.where(bottom, d, a) + mix * jnp.where(bottom, b, d)
        return carry

    lax.fori_loop(0, n // 16, enter, 0, unroll=4)
    copies = []
    for p in range(parts):

        def column(x, carry, p=p):
            base = (p * per + x) * ny
            for y in range(ny):
                at = pl.ds(pl.multiple_of((base + y) * nz, 8), nz)
                m = jnp.broadcast_to(inflow[pl.ds(base + y, 1), :], (nz, nb))
                own = jnp.concatenate([local[t, at, :] for t in range(tiles)], 1)
                stage[p, x, y] = (own + m * gain).astype(BF16)
            return carry

        if loads:
            loads[p].wait()
        if later is not None and p == 1:
            later.start()
        lax.fori_loop(0, per, column, 0)
        copy = pltpu.make_async_copy(
            stage.at[p], out_any.at[first + p * per : first + (p + 1) * per], sems.at[p]
        )
        copy.start()
        copies.append(copy)
    for copy in copies:
        copy.wait()
    if later is not None:
        later.wait()


def finish_front_kernel(
    zid_ref, fall_ref, a_ref, b_ref, d_ref, local_any, out_any, back, front, inflow, stage, sems
):
    parts = stage.shape[0]
    cut = front.shape[1]
    span = cut // parts
    loads = [
        pltpu.make_async_copy(
            local_any.at[:, p * span : (p + 1) * span],
            front.at[:, p * span : (p + 1) * span],
            sems.at[p],
        )
        for p in range(parts)
    ]
    for copy in loads:
        copy.start()
    later = pltpu.make_async_copy(local_any.at[:, cut:], back, sems.at[parts])
    given = (zid_ref, fall_ref, a_ref, b_ref, d_ref, out_any, front, inflow, stage, sems)
    finish_columns(*given, 0, loads, later)


def finish_back_kernel(
    zid_ref, fall_ref, a_ref, b_ref, d_ref, back, prev_ref, out_any, inflow, stage, sems
):
    del prev_ref
    first = out_any.shape[0] - stage.shape[0] * stage.shape[1]
    given = (zid_ref, fall_ref, a_ref, b_ref, d_ref, out_any, back, inflow, stage, sems)
    finish_columns(*given, first, [], None)


def finish_scratch(n, parts, shape):
    ny, nz, nb = shape[1:]
    return [
        pltpu.VMEM((n, nb), F32),
        pltpu.VMEM((parts, n // ny // parts, ny, nz, nb), BF16),
        pltpu.SemaphoreType.DMA((parts + 1,)),
    ]


def finish_front(zid, fall, a, b, d, local, shape, n, parts):
    nz, nb = shape[2:]
    tiles, cells, lanes = local.shape
    return pl.pallas_call(
        finish_front_kernel,
        out_shape=(
            jax.ShapeDtypeStruct(shape, BF16),
            pltpu.VMEM((tiles, cells - n * nz, lanes), F32),
        ),
        in_specs=[SMEM] + [VMEM] * 4 + [HBM],
        out_specs=(ANY, VMEM),
        scratch_shapes=[pltpu.VMEM((tiles, n * nz, lanes), F32), *finish_scratch(n, parts, shape)],
        compiler_params=pltpu.CompilerParams(vmem_limit_bytes=16 * MIB),
        name="finish_front",
    )(zid, fall, a, b, d, in_hbm(local))


def finish_back(zid, fall, a, b, d, back, prev, n, parts):
    return pl.pallas_call(
        finish_back_kernel,
        out_shape=jax.ShapeDtypeStruct(prev.shape, BF16),
        in_specs=[SMEM] + [VMEM] * 5 + [ANY],
        out_specs=ANY,
        scratch_shapes=finish_scratch(n, parts, prev.shape),
        input_output_aliases={6: 0},
        compiler_params=pltpu.CompilerParams(vmem_limit_bytes=16 * MIB),
        name="finish_back",
    )(zid, fall, a, b, d, in_vmem(back), prev)


def inner(spectrum, we, wn):
    nx, ny, nz, nb = spectrum.shape
    return pl.pallas_call(
        inner_kernel,
        out_shape=pltpu.VMEM((nb // LANES, nx * ny * nz, LANES), F32),
        in_specs=[HBM] * 3,
        out_specs=VMEM,
        scratch_shapes=[
            pltpu.VMEM(spectrum.shape, BF16),
            pltpu.VMEM(we.shape, F32),
            pltpu.VMEM(wn.shape, F32),
            pltpu.SemaphoreType.DMA((5,)),
        ],
        compiler_params=pltpu.CompilerParams(vmem_limit_bytes=8 * MIB),
        cost_estimate=pl.CostEstimate(flops=10**7, bytes_accessed=16 * MIB, transcendentals=0),
        name="inner",
    )(in_hbm(spectrum), in_hbm(we), in_hbm(wn))


def cloud(place, cells, target, adv, halo, we, wn, fall, pi, po, lk, fr, count):
    blk, blocks = cells.shape
    nb = fall.shape[1]
    return pl.pallas_call(
        cloud_kernel,
        out_shape=(
            pltpu.VMEM(adv.shape, F32),
            pltpu.VMEM((count + 4 * GAIN_ROWS, nb), BF16),
        ),
        in_specs=[SMEM, ANY, ANY] + [VMEM] * 12,
        out_specs=(VMEM, VMEM),
        scratch_shapes=[
            pltpu.SMEM((blk, blocks), jnp.int32),
            pltpu.SMEM((1, blocks), jnp.int32),
            pltpu.VMEM((nb // LANES, blk * blocks, LANES), F32),
            pltpu.SemaphoreType.DMA((2,)),
        ],
        input_output_aliases={3: 0},
        compiler_params=pltpu.CompilerParams(vmem_limit_bytes=16 * MIB),
        name="cloud",
    )(place, cells, target, in_vmem(adv), *halo, we, wn, fall, pi, po, lk, fr)


def settle(adv, fall, count):
    nb = fall.shape[1]
    return pl.pallas_call(
        settle_kernel,
        out_shape=(
            pltpu.HBM(adv.shape, F32),
            pltpu.VMEM((count + 2 * GAIN_ROWS, nb), BF16),
        ),
        in_specs=[VMEM, VMEM],
        out_specs=(HBM, VMEM),
        scratch_shapes=[pltpu.SemaphoreType.DMA((2,))],
        compiler_params=pltpu.CompilerParams(vmem_limit_bytes=4 * MIB),
        name="settle",
    )(in_vmem(adv), fall)


def body(
    spectrum,
    wind_east,
    wind_north,
    fall_rate,
    cloud_cells,
    block_target,
    pair_inputs,
    pair_outputs,
    loss_kernel,
    fragments,
):
    nx, ny, nz, nb = spectrum.shape
    n_gx, n_gy = (lax.axis_size(a) for a in ("gx", "gy"))
    up_x = [(i, (i + 1) % n_gx) for i in range(n_gx)]
    up_y = [(i, (i + 1) % n_gy) for i in range(n_gy)]
    low_x, high_x, low_y, high_y = edges(spectrum)
    south = lax.ppermute(high_y, "gy", up_y)
    north = lax.ppermute(low_y, "gy", [(b, a) for a, b in up_y])
    west = lax.ppermute(high_x, "gx", up_x)
    east = lax.ppermute(low_x, "gx", [(b, a) for a, b in up_x])

    we, wn = wind_east.transpose(0, 2, 1), wind_north.transpose(0, 2, 1)
    adv = inner(spectrum, we, wn)
    blocks, blk = cloud_cells.shape[3:]
    cells = cloud_cells.reshape(blocks, blk).T
    place = jnp.stack([lax.axis_index("gx"), lax.axis_index("gy")])
    zid = lax.axis_index("gz").reshape(1)
    columns = nx * ny
    first = 16 * ny
    adv, flux = cloud(
        place,
        cells,
        block_target,
        adv,
        (west, east, south, north),
        we,
        wn,
        fall_rate,
        pair_inputs,
        pair_outputs,
        loss_kernel,
        fragments,
        first,
    )

    def begin(flux):
        own = flux[:-GAIN_ROWS]
        a = lax.ppermute(own, "gz", [(3, 2), (2, 1)])
        b = lax.ppermute(flux, "gz", [(3, 0)])
        return own, a, b

    front = begin(flux)
    local, flux = settle(adv, fall_rate, columns - first)
    back = begin(flux)
    ready = []
    for n, (flux, a, b) in ((first, front), (columns - first, back)):
        ready.append((a, b, lax.ppermute(combine(zid, flux, a, b, n), "gz", [(1, 0), (0, 1)])))
    front, back = ready
    shape = spectrum.shape
    out, rest = finish_front(zid, fall_rate, *front, local, shape, first, 4)
    out = finish_back(zid, fall_rate, *back, rest, out, columns - first, 4)
    return out


def solution(mesh):
    in_specs = (
        P("gx", "gy", "gz", None),
        P("gx", "gy", "gz"),
        P("gx", "gy", "gz"),
        P("gz", None),
        P("gx", "gy", "gz", None, None),
        P(None, None, "gz", None),
        P(),
        P(),
        P(),
        P(),
    )
    out_specs = P("gx", "gy", "gz", None)
    return jax.shard_map(body, mesh=mesh, in_specs=in_specs, out_specs=out_specs, check_vma=False)
```

```python
import functools

import jax
import jax.numpy as jnp
from jax import lax
from jax.experimental import pallas as pl
from jax.experimental.pallas import tpu as pltpu
from jax.sharding import PartitionSpec as P

F32 = jnp.float32
BF16 = jnp.bfloat16
LANES = 128
GROUP = 8
GAIN_ROWS = 16
MIB = 2**20
VMEM = pl.BlockSpec(memory_space=pltpu.VMEM)
SMEM = pl.BlockSpec(memory_space=pltpu.SMEM)
ANY = pl.BlockSpec(memory_space=pl.ANY)
HBM = pl.BlockSpec(memory_space=pltpu.HBM)
in_hbm = functools.partial(pltpu.with_memory_space_constraint, memory_space=pltpu.HBM)
in_vmem = functools.partial(pltpu.with_memory_space_constraint, memory_space=pltpu.VMEM)


def edges_kernel(s_ref, west_ref, east_ref, south_ref, north_ref, sems):
    nx, ny = s_ref.shape[:2]
    pieces = (
        (s_ref.at[0:1], west_ref),
        (s_ref.at[nx - 1 : nx], east_ref),
        (s_ref.at[:, 0:1], south_ref),
        (s_ref.at[:, ny - 1 : ny], north_ref),
    )
    copies = [
        pltpu.make_async_copy(src, dst, sems.at[i]) for i, (src, dst) in enumerate(pieces)
    ]
    for copy in copies:
        copy.start()
    for copy in copies:
        copy.wait()


def edges(spectrum):
    nx, ny, nz, nb = spectrum.shape
    row = jax.ShapeDtypeStruct((1, ny, nz, nb), BF16)
    column = jax.ShapeDtypeStruct((nx, 1, nz, nb), BF16)
    return pl.pallas_call(
        edges_kernel,
        out_shape=(row, row, column, column),
        in_specs=[HBM],
        out_specs=[ANY] * 4,
        scratch_shapes=[pltpu.SemaphoreType.DMA((4,))],
        compiler_params=pltpu.CompilerParams(vmem_limit_bytes=MIB),
        name="edges",
    )(in_hbm(spectrum))


def wide(c, y, shape):
    return jnp.broadcast_to(c[:, y : y + 1], shape)


def inner_kernel(s_any, we_any, wn_any, adv, s_ref, we_ref, wn_ref, sems):
    nx, ny, nz, nb = s_ref.shape
    winds = [
        pltpu.make_async_copy(we_any, we_ref, sems.at[0]),
        pltpu.make_async_copy(wn_any, wn_ref, sems.at[1]),
    ]
    cuts = (0, GROUP + 1, nx // 2 + 1, nx)
    loads = [
        pltpu.make_async_copy(s_any.at[lo:hi], s_ref.at[lo:hi], sems.at[2 + i])
        for i, (lo, hi) in enumerate(zip(cuts, cuts[1:]))
    ]
    for copy in winds + loads:
        copy.start()
    for copy in winds:
        copy.wait()

    half = (nz, LANES)
    none = jnp.zeros((nz, nb), F32)

    def advect(g, carry):
        x = g * GROUP
        before, after = jnp.maximum(x - 1, 0), jnp.minimum(x + GROUP, nx - 1)
        has_before = jnp.where(x > 0, 1.0, 0.0)
        has_after = jnp.where(x + GROUP < nx, 1.0, 0.0)
        us = [we_ref[x + r] for r in range(GROUP)]
        vs = [wn_ref[x + r] for r in range(GROUP)]
        behind = [none] * GROUP
        here = [s_ref[x + r, 0].astype(F32) for r in range(GROUP)]
        for y in range(ny):
            if y < ny - 1:
                ahead = [s_ref[x + r, y + 1].astype(F32) for r in range(GROUP)]
            else:
                ahead = [none] * GROUP
            line = [
                s_ref[before, y].astype(F32) * has_before,
                *here,
                s_ref[after, y].astype(F32) * has_after,
            ]
            for r in range(GROUP):
                u, v = wide(us[r], y, half), wide(vs[r], y, half)
                from_low, from_south = u > 0.0, v > 0.0
                u, v = jnp.abs(u), jnp.abs(v)
                at = pl.ds(pl.multiple_of(((x + r) * ny + y) * nz, 8), nz)
                for t in range(nb // LANES):
                    lanes = slice(t * LANES, (t + 1) * LANES)
                    own = here[r][:, lanes]
                    side = jnp.where(from_low, line[r][:, lanes], line[r + 2][:, lanes])
                    other = jnp.where(from_south, behind[r][:, lanes], ahead[r][:, lanes])
                    adv[t, at, :] = own + u * (side - own) + v * (other - own)
            behind, here = here, ahead
        return carry

    done = 0
    for hi, copy in zip(cuts[1:], loads):
        copy.wait()
        ready = (nx if hi == nx else hi - 1) // GROUP
        lax.fori_loop(done, ready, advect, 0)
        done = ready


def settle_columns(adv, flux_ref, fall, first, count):
    nz, nb = fall.shape
    inverse = 1.0 / (1.0 + fall)
    through = fall * inverse
    tiles = adv.shape[0]

    def settle(g, carry):
        base = pl.multiple_of((first + g * 16) * nz, 128)
        for t in range(tiles):
            lanes = slice(t * LANES, (t + 1) * LANES)
            flows = []
            for half in range(2):
                inflow = jnp.zeros((8, LANES), F32)
                for z in reversed(range(nz)):
                    at = pl.ds(base + half * 8 * nz + z, 8, stride=nz)
                    total = adv[t, at, :] + inflow
                    adv[t, at, :] = total * inverse[z : z + 1, lanes]
                    inflow = total * through[z : z + 1, lanes]
                flows.append(inflow)
            flux_ref[pl.ds(pl.multiple_of(g * 16, 16), 16), lanes] = jnp.concatenate(
                flows, 0
            ).astype(BF16)
        return carry

    lax.fori_loop(0, count // 16, settle, 0, unroll=2)
    gain = jnp.ones((1, nb), F32)
    for z in reversed(range(nz)):
        gain = gain * through[z : z + 1, :]
    rest = flux_ref.shape[0] - count
    flux_ref[pl.ds(count, rest), :] = jnp.broadcast_to(gain, (rest, nb)).astype(BF16)


def cloud_kernel(
    place_ref,
    cells_any,
    target_any,
    adv_in,
    west_ref,
    east_ref,
    south_ref,
    north_ref,
    we_ref,
    wn_ref,
    fall_ref,
    pi_ref,
    po_ref,
    lk_ref,
    fr_ref,
    adv,
    flux_ref,
    cells,
    target,
    rows,
    sems,
):
    del adv_in
    nx, nz, ny = we_ref.shape
    nb = fall_ref.shape[1]
    blk, blocks = cells.shape
    pairs = po_ref.shape[0]
    tiles = nb // LANES
    plane = target_any.shape[0] * target_any.shape[1]
    lists = pltpu.make_async_copy(cells_any, cells, sems.at[0])
    routes = pltpu.make_async_copy(target_any.at[place_ref[0], place_ref[1]], target, sems.at[1])
    lists.start()
    routes.start()

    def add(cell, value):
        at = pl.ds(pl.multiple_of(cell, 8), nz)
        for t in range(tiles):
            adv[t, at, :] += value[:, t * LANES : (t + 1) * LANES]

    shape = (nz, nb)
    c_w = jnp.maximum(we_ref[0], 0.0)
    c_e = jnp.maximum(-we_ref[nx - 1], 0.0)
    for y in range(ny):
        add(y * nz, wide(c_w, y, shape) * west_ref[0, y].astype(F32))
        add(((nx - 1) * ny + y) * nz, wide(c_e, y, shape) * east_ref[0, y].astype(F32))

    def sides(i, carry):
        for k in range(4):
            x = i * 4 + k
            v = wn_ref[x]
            c_s = jnp.maximum(v, 0.0)
            c_n = jnp.maximum(-v, 0.0)
            add(x * ny * nz, wide(c_s, 0, shape) * south_ref[x, 0].astype(F32))
            add((x * ny + ny - 1) * nz, wide(c_n, ny - 1, shape) * north_ref[x, 0].astype(F32))
        return carry

    lax.fori_loop(0, nx // 4, sides, 0)
    lists.wait()

    def gather(b, carry):
        base = pl.multiple_of(b * blk, blk)
        for j in range(blk):
            for t in range(tiles):
                rows[t, pl.ds(base + j, 1), :] = adv[t, pl.ds(cells[j, b], 1), :]
        return carry

    lax.fori_loop(0, blocks, gather, 0, unroll=2)

    step = 1024
    tile = 512

    def collide(i, carry):
        here = pl.ds(pl.multiple_of(i * step, step), step)
        cloud = jnp.concatenate([rows[t, here, :] for t in range(tiles)], 1).astype(BF16)
        decline = jnp.dot(cloud, lk_ref[...], preferred_element_type=F32)
        losses = cloud.astype(F32) * decline
        total = jnp.dot(losses.astype(BF16), fr_ref[...], preferred_element_type=F32) - losses
        for n in range(pairs // tile):
            left = jnp.dot(
                cloud, pi_ref[:, n * tile : (n + 1) * tile], preferred_element_type=F32
            )
            right = jnp.dot(
                cloud,
                pi_ref[:, pairs + n * tile : pairs + (n + 1) * tile],
                preferred_element_type=F32,
            )
            total = total + jnp.dot(
                (left * right).astype(BF16),
                po_ref[n * tile : (n + 1) * tile, :],
                preferred_element_type=F32,
            )
        total = total.astype(BF16).astype(F32)
        for t in range(tiles):
            rows[t, here, :] += total[:, t * LANES : (t + 1) * LANES]
        return carry

    lax.fori_loop(0, blocks * blk // step, collide, 0)
    routes.wait()

    def scatter(b, carry):
        base = pl.multiple_of(b * blk, blk)

        @pl.when(target[0, b] < plane)
        def _():
            for j in range(blk):
                for t in range(tiles):
                    adv[t, pl.ds(cells[j, b], 1), :] = rows[t, pl.ds(base + j, 1), :]

        return carry

    lax.fori_loop(0, blocks, scatter, 0, unroll=4)
    count = flux_ref.shape[0] - 4 * GAIN_ROWS
    settle_columns(adv, flux_ref, fall_ref[...], 0, count)


def settle_kernel(adv, fall_ref, local_any, flux_ref, sems):
    nz = fall_ref.shape[0]
    count = flux_ref.shape[0] - 2 * GAIN_ROWS
    first = adv.shape[1] // nz - count
    cut = first * nz
    front = pltpu.make_async_copy(adv.at[:, :cut], local_any.at[:, :cut], sems.at[0])
    back = pltpu.make_async_copy(adv.at[:, cut:], local_any.at[:, cut:], sems.at[1])
    front.start()
    settle_columns(adv, flux_ref, fall_ref[...], first, count)
    back.start()
    front.wait()
    back.wait()


def combine_kernel(zid_ref, own_ref, a_ref, b_ref, out_ref, *, n):
    z = zid_ref[0]

    @pl.when(z == 0)
    def _():
        out_ref[...] = b_ref[0 : own_ref.shape[0], :]

    @pl.when(z != 0)
    def _():
        gain = own_ref[n : n + GAIN_ROWS, :].astype(F32)

        def some(i, carry):
            at = pl.ds(pl.multiple_of(i * 16, 16), 16)
            out_ref[at, :] = (
                own_ref[at, :].astype(F32) + gain * a_ref[at, :].astype(F32)
            ).astype(BF16)
            return carry

        lax.fori_loop(0, n // 16, some, 0, unroll=4)
        for row in range(n, own_ref.shape[0], GAIN_ROWS):
            at = slice(row, row + GAIN_ROWS)
            out_ref[at, :] = (gain * a_ref[at, :].astype(F32)).astype(BF16)


def combine(zid, own, a, b, n):
    return pl.pallas_call(
        functools.partial(combine_kernel, n=n),
        out_shape=pltpu.VMEM(own.shape, BF16),
        in_specs=[SMEM] + [VMEM] * 3,
        out_specs=VMEM,
        compiler_params=pltpu.CompilerParams(vmem_limit_bytes=4 * MIB),
        name="combine",
    )(zid, own, a, b)


def finish_columns(
    zid_ref, fall_ref, a_ref, b_ref, d_ref, out_any, local, inflow, stage, sems, first, loads, later
):
    ny, nz, nb = out_any.shape[1:]
    parts, per = stage.shape[:2]
    tiles = nb // LANES
    n = inflow.shape[0]
    fall = fall_ref[...]
    inverse = 1.0 / (1.0 + fall)
    through = fall * inverse
    carried = jnp.ones((1, nb), F32)
    gains = [None] * nz
    for level in reversed(range(nz)):
        gains[level] = carried * inverse[level : level + 1, :]
        carried = carried * through[level : level + 1, :]
    gain = jnp.concatenate(gains, 0)
    bottom = zid_ref[0] == 0
    mix = jnp.where(bottom, d_ref[n : n + GAIN_ROWS, :], a_ref[n : n + GAIN_ROWS, :]).astype(F32)

    def enter(i, carry):
        at = pl.ds(pl.multiple_of(i * 16, 16), 16)
        a, b, d = a_ref[at, :].astype(F32), b_ref[at, :].astype(F32), d_ref[at, :].astype(F32)
        inflow[at, :] = jnp.where(bottom, d, a) + mix * jnp.where(bottom, b, d)
        return carry

    lax.fori_loop(0, n // 16, enter, 0, unroll=4)
    copies = []
    for p in range(parts):

        def column(x, carry, p=p):
            base = (p * per + x) * ny
            for y in range(ny):
                at = pl.ds(pl.multiple_of((base + y) * nz, 8), nz)
                m = jnp.broadcast_to(inflow[pl.ds(base + y, 1), :], (nz, nb))
                own = jnp.concatenate([local[t, at, :] for t in range(tiles)], 1)
                stage[p, x, y] = (own + m * gain).astype(BF16)
            return carry

        if loads:
            loads[p].wait()
        if later is not None and p == 1:
            later.start()
        lax.fori_loop(0, per, column, 0)
        copy = pltpu.make_async_copy(
            stage.at[p], out_any.at[first + p * per : first + (p + 1) * per], sems.at[p]
        )
        copy.start()
        copies.append(copy)
    for copy in copies:
        copy.wait()
    if later is not None:
        later.wait()


def finish_front_kernel(
    zid_ref, fall_ref, a_ref, b_ref, d_ref, local_any, out_any, back, front, inflow, stage, sems
):
    parts = stage.shape[0]
    cut = front.shape[1]
    span = cut // parts
    loads = [
        pltpu.make_async_copy(
            local_any.at[:, p * span : (p + 1) * span],
            front.at[:, p * span : (p + 1) * span],
            sems.at[p],
        )
        for p in range(parts)
    ]
    for copy in loads:
        copy.start()
    later = pltpu.make_async_copy(local_any.at[:, cut:], back, sems.at[parts])
    given = (zid_ref, fall_ref, a_ref, b_ref, d_ref, out_any, front, inflow, stage, sems)
    finish_columns(*given, 0, loads, later)


def finish_back_kernel(
    zid_ref, fall_ref, a_ref, b_ref, d_ref, back, prev_ref, out_any, inflow, stage, sems
):
    del prev_ref
    first = out_any.shape[0] - stage.shape[0] * stage.shape[1]
    given = (zid_ref, fall_ref, a_ref, b_ref, d_ref, out_any, back, inflow, stage, sems)
    finish_columns(*given, first, [], None)


def finish_scratch(n, parts, shape):
    ny, nz, nb = shape[1:]
    return [
        pltpu.VMEM((n, nb), F32),
        pltpu.VMEM((parts, n // ny // parts, ny, nz, nb), BF16),
        pltpu.SemaphoreType.DMA((parts + 1,)),
    ]


def finish_front(zid, fall, a, b, d, local, shape, n, parts):
    nz, nb = shape[2:]
    tiles, cells, lanes = local.shape
    return pl.pallas_call(
        finish_front_kernel,
        out_shape=(
            jax.ShapeDtypeStruct(shape, BF16),
            pltpu.VMEM((tiles, cells - n * nz, lanes), F32),
        ),
        in_specs=[SMEM] + [VMEM] * 4 + [HBM],
        out_specs=(ANY, VMEM),
        scratch_shapes=[pltpu.VMEM((tiles, n * nz, lanes), F32), *finish_scratch(n, parts, shape)],
        compiler_params=pltpu.CompilerParams(vmem_limit_bytes=16 * MIB),
        name="finish_front",
    )(zid, fall, a, b, d, in_hbm(local))


def finish_back(zid, fall, a, b, d, back, prev, n, parts):
    return pl.pallas_call(
        finish_back_kernel,
        out_shape=jax.ShapeDtypeStruct(prev.shape, BF16),
        in_specs=[SMEM] + [VMEM] * 5 + [ANY],
        out_specs=ANY,
        scratch_shapes=finish_scratch(n, parts, prev.shape),
        input_output_aliases={6: 0},
        compiler_params=pltpu.CompilerParams(vmem_limit_bytes=16 * MIB),
        name="finish_back",
    )(zid, fall, a, b, d, in_vmem(back), prev)


def inner(spectrum, we, wn):
    nx, ny, nz, nb = spectrum.shape
    return pl.pallas_call(
        inner_kernel,
        out_shape=pltpu.VMEM((nb // LANES, nx * ny * nz, LANES), F32),
        in_specs=[HBM] * 3,
        out_specs=VMEM,
        scratch_shapes=[
            pltpu.VMEM(spectrum.shape, BF16),
            pltpu.VMEM(we.shape, F32),
            pltpu.VMEM(wn.shape, F32),
            pltpu.SemaphoreType.DMA((5,)),
        ],
        compiler_params=pltpu.CompilerParams(vmem_limit_bytes=8 * MIB),
        cost_estimate=pl.CostEstimate(flops=10**7, bytes_accessed=16 * MIB, transcendentals=0),
        name="inner",
    )(in_hbm(spectrum), in_hbm(we), in_hbm(wn))


def cloud(place, cells, target, adv, halo, we, wn, fall, pi, po, lk, fr, count):
    blk, blocks = cells.shape
    nb = fall.shape[1]
    return pl.pallas_call(
        cloud_kernel,
        out_shape=(
            pltpu.VMEM(adv.shape, F32),
            pltpu.VMEM((count + 4 * GAIN_ROWS, nb), BF16),
        ),
        in_specs=[SMEM, ANY, ANY] + [VMEM] * 12,
        out_specs=(VMEM, VMEM),
        scratch_shapes=[
            pltpu.SMEM((blk, blocks), jnp.int32),
            pltpu.SMEM((1, blocks), jnp.int32),
            pltpu.VMEM((nb // LANES, blk * blocks, LANES), F32),
            pltpu.SemaphoreType.DMA((2,)),
        ],
        input_output_aliases={3: 0},
        compiler_params=pltpu.CompilerParams(vmem_limit_bytes=16 * MIB),
        name="cloud",
    )(place, cells, target, in_vmem(adv), *halo, we, wn, fall, pi, po, lk, fr)


def settle(adv, fall, count):
    nb = fall.shape[1]
    return pl.pallas_call(
        settle_kernel,
        out_shape=(
            pltpu.HBM(adv.shape, F32),
            pltpu.VMEM((count + 2 * GAIN_ROWS, nb), BF16),
        ),
        in_specs=[VMEM, VMEM],
        out_specs=(HBM, VMEM),
        scratch_shapes=[pltpu.SemaphoreType.DMA((2,))],
        compiler_params=pltpu.CompilerParams(vmem_limit_bytes=4 * MIB),
        name="settle",
    )(in_vmem(adv), fall)


def body(
    spectrum,
    wind_east,
    wind_north,
    fall_rate,
    cloud_cells,
    block_target,
    pair_inputs,
    pair_outputs,
    loss_kernel,
    fragments,
):
    nx, ny, nz, nb = spectrum.shape
    n_gx, n_gy = (lax.axis_size(a) for a in ("gx", "gy"))
    up_x = [(i, (i + 1) % n_gx) for i in range(n_gx)]
    up_y = [(i, (i + 1) % n_gy) for i in range(n_gy)]
    low_x, high_x, low_y, high_y = edges(spectrum)
    south = lax.ppermute(high_y, "gy", up_y)
    north = lax.ppermute(low_y, "gy", [(b, a) for a, b in up_y])
    west = lax.ppermute(high_x, "gx", up_x)
    east = lax.ppermute(low_x, "gx", [(b, a) for a, b in up_x])

    we, wn = wind_east.transpose(0, 2, 1), wind_north.transpose(0, 2, 1)
    adv = inner(spectrum, we, wn)
    blocks, blk = cloud_cells.shape[3:]
    cells = cloud_cells.reshape(blocks, blk).T
    place = jnp.stack([lax.axis_index("gx"), lax.axis_index("gy")])
    zid = lax.axis_index("gz").reshape(1)
    columns = nx * ny
    first = 16 * ny
    adv, flux = cloud(
        place,
        cells,
        block_target,
        adv,
        (west, east, south, north),
        we,
        wn,
        fall_rate,
        pair_inputs,
        pair_outputs,
        loss_kernel,
        fragments,
        first,
    )

    def begin(flux):
        own = flux[:-GAIN_ROWS]
        a = lax.ppermute(own, "gz", [(3, 2), (2, 1)])
        b = lax.ppermute(flux, "gz", [(3, 0)])
        return own, a, b

    front = begin(flux)
    local, flux = settle(adv, fall_rate, columns - first)
    back = begin(flux)
    ready = []
    for n, (flux, a, b) in ((first, front), (columns - first, back)):
        ready.append((a, b, lax.ppermute(combine(zid, flux, a, b, n), "gz", [(1, 0), (0, 1)])))
    front, back = ready
    shape = spectrum.shape
    out, rest = finish_front(zid, fall_rate, *front, local, shape, first, 4)
    out = finish_back(zid, fall_rate, *back, rest, out, columns - first, 8)
    return out


def solution(mesh):
    in_specs = (
        P("gx", "gy", "gz", None),
        P("gx", "gy", "gz"),
        P("gx", "gy", "gz"),
        P("gz", None),
        P("gx", "gy", "gz", None, None),
        P(None, None, "gz", None),
        P(),
        P(),
        P(),
        P(),
    )
    out_specs = P("gx", "gy", "gz", None)
    return jax.shard_map(body, mesh=mesh, in_specs=in_specs, out_specs=out_specs, check_vma=False)
```
